1024 devices in a mesh: dp: 16 (over y, x_lo), expert: 64 (over x_hi, z, core).
Axes of the slice: x: 4 (x_hi: 2, x_lo: 2; x = x_hi * 2 + x_lo), y: 8, z: 16, core: 2. Of those that a mesh axis runs over, the one named last changes fastest.
Arguments:
- tokens: bfloat16 [1024, 256, 1280], P(('dp', 'expert')), may hold values from -16 to 16
- cotangent: bfloat16 [1024, 256, 1280], P(('dp', 'expert')), may hold values from -6 to 6
- slot_params: bfloat16 [1280, 8], replicated, may hold values from -1 to 1
- in_weight: bfloat16 [1280, 40960], P(None, 'expert'), may hold values from -0.15625 to 0.15625
- out_weight: bfloat16 [1280, 40960], P(None, 'expert'), may hold values from -0.078125 to 0.078125
Outputs:
- mixed: bfloat16 [1024, 256, 1280], P(('dp', 'expert'))
- grad_tokens: bfloat16 [1024, 256, 1280], P(('dp', 'expert'))
- grad_in_weight: float32 [1280, 40960], P('dp', 'expert')
- grad_out_weight: float32 [1280, 40960], P('dp', 'expert')
The draws below stay inside these ranges and needn't reach their ends.
All inputs are finite; a program needn't handle non-finite values.
Results may differ from the reference program's by a relative error of at most 0.022.
Values may be sent and summed in bfloat16 or wider, within the bound.
No kernel may reach another device: no remote copies, remote signals or barrier semaphores. Data moves between devices by JAX's collectives and lax.ppermute only.
A program may use at most 32 MiB of HBM per device.

```python
import math
import jax
import jax.numpy as jnp
from jax import lax

D = 1280
FF = 5120
PATCH = 256
SHARDS = 8
FF_DEV = 640
EXPERTS = 8
IMAGES = 1024
N_DP = 16


def shared_columns(key):
    values = jnp.clip(jax.random.normal(key, (D, EXPERTS), jnp.float32), -6.0, 6.0)
    return jnp.clip(values * (3.0 / math.sqrt(D)), -1.0, 1.0)


def draw_slot_params(key, part):
    columns = shared_columns(key)
    return columns.astype(jnp.bfloat16)


def draw_tokens(key, part):
    key = jax.random.fold_in(key, 3)
    keys = jax.random.split(key, 1)
    shape = (IMAGES, PATCH, D)
    result = jnp.clip(jax.random.normal(keys[0], shape, jnp.float32), -6.0, 6.0)
    return jnp.clip(result, -16.0, 16.0).astype(jnp.bfloat16)


def levels(rng, dims, cuts, least, high):
    def one(dim, blocks):
        draws = jax.random.uniform(jax.random.fold_in(jax.random.fold_in(rng, 6), dim), (blocks,), jnp.float32, least / len(cuts), high / len(cuts))
        return jnp.repeat(jnp.exp(draws), dims[dim] // blocks).reshape((-1,) + (1,) * (len(dims) - dim - 1))

    loudness = one(*cuts[0])
    for cut in cuts[1:]:
        loudness = loudness * one(*cut)
    return loudness


def scatter_about(stream_key, dims, scale, reach, cuts=(), kind=jnp.bfloat16):
    values = scale * jax.random.normal(stream_key, dims, jnp.float32)
    if cuts:
        values = values * levels(stream_key, dims, cuts, -0.22, 0.18)
    return jnp.clip(values, -reach, reach).astype(kind)


def setup_inputs(seed: int = 0) -> dict:
    key_of = jax.random.split(jax.random.key(seed), 6)
    tokens = draw_tokens(jax.random.fold_in(key_of[5], 71), 0)
    cotangent = scatter_about(key_of[1], (IMAGES, PATCH, D), 1.0, 6.0, ((0, 1024),))
    slot_params = draw_slot_params(jax.random.fold_in(key_of[5], 71), 0)
    in_weight = scatter_about(key_of[3], (D, EXPERTS * FF), D ** -0.5, 0.15625, ((1, 64),))
    out_weight = scatter_about(key_of[4], (D, EXPERTS * FF), FF ** -0.5, 0.078125, ((1, 64),))
    return {"tokens": tokens, "cotangent": cotangent, "slot_params": slot_params, "in_weight": in_weight, "out_weight": out_weight}


root_half = 0.7071067811865476
density = 0.3989422804014327


def gelu_parts(preact):
    cumulative = 0.5 * (1.0 + lax.erf(preact * root_half))
    return preact * cumulative, cumulative + preact * jnp.exp(-0.5 * preact * preact) * density


def group_sum(left, right):
    left_groups = left.reshape(N_DP, -1, left.shape[1]).astype(jnp.float32)
    right_groups = right.reshape(N_DP, -1, right.shape[1]).astype(jnp.float32)
    partial_sums = jnp.einsum("pgd,pgf->pdf", left_groups, right_groups, precision=lax.Precision.HIGHEST)
    rounded = lax.optimization_barrier(partial_sums.astype(jnp.bfloat16))
    return jnp.sum(rounded.astype(jnp.float32), axis=0)


def add_blocks(parts):
    rounded = lax.optimization_barrier(parts)
    return jnp.sum(rounded.astype(jnp.float32), axis=0).astype(jnp.bfloat16)


def reference(tokens, cotangent, slot_params, in_weight, out_weight):
    def route(pack):
        image_rows, grad_rows = pack
        logits = jnp.dot(image_rows, slot_params, preferred_element_type=jnp.float32)
        dispatch = jax.nn.softmax(logits, axis=0).astype(jnp.bfloat16)
        combine = jax.nn.softmax(logits, axis=1).astype(jnp.bfloat16)
        slot_in = jnp.dot(dispatch.T, image_rows, preferred_element_type=jnp.float32).astype(jnp.bfloat16)
        slot_grad = jnp.dot(combine.T, grad_rows, preferred_element_type=jnp.float32).astype(jnp.bfloat16)
        return slot_in, slot_grad

    slot_in, slot_grad = lax.map(route, (tokens, cotangent))

    in_blocks = in_weight.reshape(D, EXPERTS, SHARDS, FF_DEV).transpose(1, 2, 0, 3)
    out_blocks = out_weight.reshape(D, EXPERTS, SHARDS, FF_DEV).transpose(1, 2, 0, 3)

    def one_expert(pack):
        rows_in, rows_grad, in_set, out_set = pack

        def one_block(weights):
            in_block, out_block = weights
            preact = jnp.dot(rows_in, in_block, preferred_element_type=jnp.float32)
            activation, slope = gelu_parts(preact)
            activated = activation.astype(jnp.bfloat16)
            out_part = jnp.dot(activated, out_block.T, preferred_element_type=jnp.float32).astype(jnp.bfloat16)
            grad_hidden = jnp.dot(rows_grad, out_block, preferred_element_type=jnp.float32)
            grad_preact = (grad_hidden * slope).astype(jnp.bfloat16)
            grad_part = jnp.dot(grad_preact, in_block.T, preferred_element_type=jnp.float32).astype(jnp.bfloat16)
            return out_part, grad_part, group_sum(rows_in, grad_preact), group_sum(rows_grad, activated)

        out_parts, grad_parts, grad_in_set, grad_out_set = lax.map(one_block, (in_set, out_set))
        return add_blocks(out_parts), add_blocks(grad_parts), grad_in_set, grad_out_set

    slot_out, grad_slot_in, grad_in_sets, grad_out_sets = lax.map(
        one_expert, (slot_in.transpose(1, 0, 2), slot_grad.transpose(1, 0, 2), in_blocks, out_blocks))

    def finish(pack):
        image_rows, grad_rows, outputs, slot_grads = pack
        logits = jnp.dot(image_rows, slot_params, preferred_element_type=jnp.float32)
        dispatch_soft = jax.nn.softmax(logits, axis=0)
        combine_soft = jax.nn.softmax(logits, axis=1)
        dispatch = dispatch_soft.astype(jnp.bfloat16)
        combine = combine_soft.astype(jnp.bfloat16)
        mixed = jnp.dot(combine, outputs, preferred_element_type=jnp.float32).astype(jnp.bfloat16)
        combine_grad = jnp.dot(grad_rows, outputs.T, preferred_element_type=jnp.float32)
        dispatch_grad = jnp.dot(image_rows, slot_grads.T, preferred_element_type=jnp.float32)
        logit_grad = combine_soft * (combine_grad - jnp.sum(combine_soft * combine_grad, axis=1, keepdims=True))
        logit_grad = logit_grad + dispatch_soft * (dispatch_grad - jnp.sum(dispatch_soft * dispatch_grad, axis=0, keepdims=True))
        logit_grad = logit_grad.astype(jnp.bfloat16)
        grad_tokens = jnp.dot(dispatch, slot_grads, preferred_element_type=jnp.float32)
        grad_tokens = grad_tokens + jnp.dot(logit_grad, slot_params.T, preferred_element_type=jnp.float32)
        return mixed, grad_tokens.astype(jnp.bfloat16)

    mixed, grad_tokens = lax.map(
        finish, (tokens, cotangent, slot_out.transpose(1, 0, 2), grad_slot_in.transpose(1, 0, 2)))
    grad_in_weight = grad_in_sets.transpose(2, 0, 1, 3).reshape(D, EXPERTS * SHARDS * FF_DEV)
    grad_out_weight = grad_out_sets.transpose(2, 0, 1, 3).reshape(D, EXPERTS * SHARDS * FF_DEV)
    return mixed, grad_tokens, grad_in_weight, grad_out_weight
```

```python
import functools

import jax
import jax.numpy as jnp
import numpy as np
from jax import lax
from jax.experimental import pallas as pl
from jax.experimental.pallas import tpu as pltpu
from jax.sharding import Mesh
from jax.sharding import PartitionSpec as P

root_half = 0.7071067811865476
density = 0.3989422804014327
f32 = jnp.float32
bf16 = jnp.bfloat16

AXES = ("yh", "yl", "xl", "xh", "zh", "zl", "c")
SIZES = (4, 2, 2, 2, 4, 4, 2)
DP = ("yh", "yl", "xl")
PEERS = ("xh", "zh", "zl", "c")
CHIPS = ("xh", "zh", "zl")
QUAD = ("yl", "xl")
EXPERTS, SPREAD, CHIP_COUNT = 8, 4, 32
QUADS = 4
VMEM = 48 * 1024 * 1024


def nn(a, b):
    return lax.dot_general(a, b, (((1,), (0,)), ((), ())), preferred_element_type=f32)


def nt(a, b):
    return lax.dot_general(a, b, (((1,), (1,)), ((), ())), preferred_element_type=f32)


def tn(a, b):
    return lax.dot_general(a, b, (((0,), (0,)), ((), ())), preferred_element_type=f32)


def pick(rows, cols, source):
    r = lax.broadcasted_iota(jnp.int32, (rows, cols), 0)
    c = lax.broadcasted_iota(jnp.int32, (rows, cols), 1)
    return jnp.where(c == source(r), 1.0, 0.0).astype(bf16)


def call(kernel, outs, flops, nbytes, scratch=(), smem=0, ins=1):
    vm = pl.BlockSpec(memory_space=pltpu.VMEM)
    specs = [pl.BlockSpec(memory_space=pltpu.SMEM)] * smem + [vm] * (ins - smem)
    return pl.pallas_call(
        kernel,
        out_shape=[jax.ShapeDtypeStruct(s, d) for s, d in outs],
        in_specs=specs,
        out_specs=[vm] * len(outs),
        scratch_shapes=list(scratch),
        compiler_params=pltpu.CompilerParams(vmem_limit_bytes=VMEM),
        cost_estimate=pl.CostEstimate(flops=flops, bytes_accessed=nbytes, transcendentals=0),
    )


def route_kernel(tok, cot, sp, send, disp, comb):
    logits = nt(sp[...], tok[...])
    ed = jnp.exp(logits - jnp.max(logits, axis=1, keepdims=True))
    d = ed / jnp.sum(ed, axis=1, keepdims=True)
    ec = jnp.exp(logits - jnp.max(logits, axis=0, keepdims=True))
    c = ec / jnp.sum(ec, axis=0, keepdims=True)
    disp[...] = d
    comb[...] = c
    slot_in = nn(d.astype(bf16), tok[...]).astype(bf16)
    slot_grad = nn(c.astype(bf16), cot[...]).astype(bf16)
    both = jnp.concatenate([slot_in.astype(f32), slot_grad.astype(f32)], axis=0).astype(bf16)
    rows = 2 * CHIP_COUNT
    sel = pick(rows, 16, lambda r: (r % 2) * EXPERTS + r // (2 * SPREAD))
    send[...] = nn(sel, both).astype(bf16)


def expert_kernel(place, own, other, w_in, w_out, part_own, part_other, c0, c1, c2, c3, turned):
    n = own.shape[0] // 2
    even = pick(n, 2 * n, lambda r: 2 * r)
    odd = pick(n, 2 * n, lambda r: 2 * r + 1)
    rows_in = jnp.concatenate([nn(even, own[...]), nn(even, other[...])], axis=0).astype(bf16)
    rows_grad = jnp.concatenate([nn(odd, own[...]), nn(odd, other[...])], axis=0).astype(bf16)
    preact = nn(rows_in, w_in[...])
    hidden_grad = nn(rows_grad, w_out[...])
    cumulative = 0.5 * (1.0 + lax.erf(preact * root_half))
    slope = cumulative + preact * jnp.exp(-0.5 * preact * preact) * density
    act = (preact * cumulative).astype(bf16)
    gp = (hidden_grad * slope).astype(bf16)
    out_part = nt(act, w_out[...]).astype(bf16)
    grad_part = nt(gp, w_in[...]).astype(bf16)
    part_own[...] = (tn(even, out_part[:n]) + tn(odd, grad_part[:n])).astype(bf16)
    part_other[...] = (tn(even, out_part[n:]) + tn(odd, grad_part[n:])).astype(bf16)
    both = jnp.concatenate([rows_in, rows_grad], axis=0)
    turned[...] = jnp.transpose(both.astype(f32)).astype(bf16)
    yh, j0 = place[0], place[1]
    depth = turned.shape[0] // 16
    for m, chunk in enumerate((c0, c1, c2, c3)):
        chunk[0 : 2 * n, :] = gp
        chunk[2 * n : 4 * n, :] = act
        j = jnp.bitwise_xor(j0, m)
        pieces = []
        for k in range(4):
            at = (lax.rem(yh + k, 4) * QUADS + j) * depth
            pieces.append(turned[pl.ds(pl.multiple_of(at, 16), depth), :])
        piece = jnp.concatenate(pieces, axis=0)
        for b in range(5):
            chunk[4 * n : 6 * n, 128 * b : 128 * (b + 1)] = piece[64 * b : 64 * (b + 1)]


def term_kernel(c0, c1, c2, c3, keep, s1, s2, s3):
    left, right = [], []
    zero = jnp.zeros((64, 640), bf16)
    for chunk in (c0, c1, c2, c3):
        left.append(jnp.concatenate([chunk[128:192, 128 * b : 128 * (b + 1)] for b in range(5)], axis=0))
        right.append(jnp.concatenate([chunk[0:64, :], zero], axis=1))
        right.append(jnp.concatenate([zero, chunk[64:128, :]], axis=1))
    total = nn(jnp.concatenate(left, axis=1), jnp.concatenate(right, axis=0))
    depth = keep.shape[0]
    keep[...] = total[:depth]
    for k, s in enumerate((s1, s2, s3)):
        s[...] = total[(k + 1) * depth : (k + 2) * depth].astype(bf16)


def finish_kernel(tok, cot, sp, parts, disp, comb, mixed, grad_tokens):
    r = lax.broadcasted_iota(jnp.int32, (16, 2 * CHIP_COUNT), 0)
    c = lax.broadcasted_iota(jnp.int32, (16, 2 * CHIP_COUNT), 1)
    sel = jnp.where(((c % 2) * EXPERTS + c // (2 * SPREAD)) == r, 1.0, 0.0).astype(bf16)
    slots = nn(sel, parts[...])
    slot_out = slots[:8].astype(bf16)
    grad_slot_in = slots[8:].astype(bf16)
    d, cm = disp[...], comb[...]
    mixed[...] = tn(cm.astype(bf16), slot_out).astype(bf16)
    combine_grad = nt(slot_out, cot[...])
    dispatch_grad = nt(grad_slot_in, tok[...])
    lg = cm * (combine_grad - jnp.sum(cm * combine_grad, axis=0, keepdims=True))
    lg = lg + d * (dispatch_grad - jnp.sum(d * dispatch_grad, axis=1, keepdims=True))
    rows = jnp.concatenate([d.astype(bf16).astype(f32), lg.astype(bf16).astype(f32)], axis=0)
    cols = jnp.concatenate([grad_slot_in.astype(f32), sp[...].astype(f32)], axis=0)
    grad_tokens[...] = tn(rows.astype(bf16), cols.astype(bf16)).astype(bf16)


def per_device(tokens, cotangent, slot_params, in_weight, out_weight):
    tok, cot = tokens[0], cotangent[0]
    patch, width = tok.shape
    hidden = in_weight.shape[1]
    sp = slot_params.T
    n2 = 2 * CHIP_COUNT
    send, disp, comb = call(
        route_kernel,
        [((n2, width), bf16), ((EXPERTS, patch), f32), ((EXPERTS, patch), f32)],
        10**7, 1500000, ins=3,
    )(tok, cot, sp)

    def exchange(rows):
        got = lax.all_to_all(rows.reshape(CHIP_COUNT, 2, width), CHIPS, 0, 0, tiled=True)
        return got.reshape(n2, width)

    swap = [(0, 1), (1, 0)]
    own = exchange(send)
    other = lax.ppermute(own, "c", swap)
    place = jnp.stack([lax.axis_index("yh"), lax.axis_index(QUAD)]).astype(jnp.int32)
    chunk_shape = ((192, hidden), bf16)
    part_own, part_other, c0, c1, c2, c3 = call(
        expert_kernel,
        [((n2, width), bf16), ((n2, width), bf16)] + [chunk_shape] * 4,
        5 * 10**8, 4500000, scratch=[pltpu.VMEM((width, 128), bf16)], smem=1, ins=5,
    )(place, own, other, in_weight, out_weight)

    back = lax.ppermute(part_other, "c", swap)
    got = [c0]
    for m, chunk in ((1, c1), (2, c2), (3, c3)):
        got.append(lax.ppermute(chunk, QUAD, [(i, i ^ m) for i in range(QUADS)]))
    parts = exchange((part_own.astype(f32) + back.astype(f32)).astype(bf16))

    depth = width // 16
    piece = ((depth, 2 * hidden), bf16)
    keep, s1, s2, s3 = call(
        term_kernel,
        [((depth, 2 * hidden), f32), piece, piece, piece],
        4 * 10**8, 2500000, ins=4,
    )(*got)
    total = keep
    for k, s in ((1, s1), (2, s2), (3, s3)):
        total = total + lax.ppermute(s, "yh", [(i, (i + k) % 4) for i in range(4)]).astype(f32)

    mixed, grad_tokens = call(
        finish_kernel,
        [((patch, width), bf16), ((patch, width), bf16)],
        3 * 10**7, 3000000, ins=6,
    )(tok, cot, sp, parts, disp, comb)
    return mixed[None], grad_tokens[None], total[:, :hidden], total[:, hidden:]


def solution(mesh):
    fine = Mesh(np.asarray(mesh.devices).reshape(SIZES), AXES)
    return jax.shard_map(
        per_device,
        mesh=fine,
        in_specs=(P(AXES), P(AXES), P(), P(None, PEERS), P(None, PEERS)),
        out_specs=(P(AXES), P(AXES), P(DP, PEERS), P(DP, PEERS)),
        check_vma=False,
    )
```

```python
import functools

import jax
import jax.numpy as jnp
import numpy as np
from jax import lax
from jax.experimental import pallas as pl
from jax.experimental.pallas import tpu as pltpu
from jax.sharding import Mesh
from jax.sharding import PartitionSpec as P

root_half = 0.7071067811865476
density = 0.3989422804014327
f32 = jnp.float32
bf16 = jnp.bfloat16

AXES = ("yh", "yl", "xl", "xh", "zh", "zl", "c")
SIZES = (4, 2, 2, 2, 4, 4, 2)
DP = ("yh", "yl", "xl")
PEERS = ("xh", "zh", "zl", "c")
CHIPS = ("xh", "zh", "zl")
QUAD = ("yl", "xl")
EXPERTS, SPREAD, CHIP_COUNT = 8, 4, 32
QUADS = 4
ROOM = 20_000_000


def nn(a, b):
    return lax.dot_general(a, b, (((1,), (0,)), ((), ())), preferred_element_type=f32)


def nt(a, b):
    return lax.dot_general(a, b, (((1,), (1,)), ((), ())), preferred_element_type=f32)


def tn(a, b):
    return lax.dot_general(a, b, (((0,), (0,)), ((), ())), preferred_element_type=f32)


def pick(rows, cols, source):
    r = lax.broadcasted_iota(jnp.int32, (rows, cols), 0)
    c = lax.broadcasted_iota(jnp.int32, (rows, cols), 1)
    return jnp.where(c == source(r), 1.0, 0.0).astype(bf16)


def call(kernel, outs, flops, nbytes, ins, scratch=(), room=ROOM):
    vm = pl.BlockSpec(memory_space=pltpu.VMEM)
    spaces = {"v": vm, "s": pl.BlockSpec(memory_space=pltpu.SMEM), "a": pl.BlockSpec(memory_space=pl.ANY)}
    spaces["h"] = pl.BlockSpec(memory_space=pltpu.HBM)
    specs = [spaces[letter] for letter in ins]
    return pl.pallas_call(
        kernel,
        out_shape=[jax.ShapeDtypeStruct(s, d) for s, d in outs],
        in_specs=specs,
        out_specs=[vm] * len(outs),
        scratch_shapes=list(scratch),
        compiler_params=pltpu.CompilerParams(vmem_limit_bytes=room),
        cost_estimate=pl.CostEstimate(flops=flops, bytes_accessed=nbytes, transcendentals=0),
    )


def route_kernel(tok_hbm, cot_hbm, sp, send, disp, comb, tok, cot, sems):
    copy_tok = pltpu.make_async_copy(tok_hbm, tok, sems.at[0])
    copy_cot = pltpu.make_async_copy(cot_hbm, cot, sems.at[1])
    copy_tok.start()
    copy_cot.start()
    copy_tok.wait()
    logits = nt(sp[...], tok[...])
    ed = jnp.exp(logits - jnp.max(logits, axis=1, keepdims=True))
    d = ed / jnp.sum(ed, axis=1, keepdims=True)
    ec = jnp.exp(logits - jnp.max(logits, axis=0, keepdims=True))
    c = ec / jnp.sum(ec, axis=0, keepdims=True)
    disp[...] = d
    comb[...] = c
    slot_in = nn(d.astype(bf16), tok[...]).astype(bf16)
    copy_cot.wait()
    slot_grad = nn(c.astype(bf16), cot[...]).astype(bf16)
    both = jnp.concatenate([slot_in.astype(f32), slot_grad.astype(f32)], axis=0).astype(bf16)
    rows = 2 * CHIP_COUNT
    sel = pick(rows, 16, lambda r: (r % 2) * EXPERTS + r // (2 * SPREAD))
    send[...] = nn(sel, both).astype(bf16)


def expert_kernel(place, own, other, w_in, w_out, part_own, part_other, c0, c1, c2, c3, turned):
    n = own.shape[0] // 2
    even = pick(n, 2 * n, lambda r: 2 * r)
    odd = pick(n, 2 * n, lambda r: 2 * r + 1)
    rows_in = jnp.concatenate([nn(even, own[...]), nn(even, other[...])], axis=0).astype(bf16)
    rows_grad = jnp.concatenate([nn(odd, own[...]), nn(odd, other[...])], axis=0).astype(bf16)
    preact = nn(rows_in, w_in[...])
    hidden_grad = nn(rows_grad, w_out[...])
    cumulative = 0.5 * (1.0 + lax.erf(preact * root_half))
    slope = cumulative + preact * jnp.exp(-0.5 * preact * preact) * density
    act = (preact * cumulative).astype(bf16)
    gp = (hidden_grad * slope).astype(bf16)
    out_part = nt(act, w_out[...]).astype(bf16)
    grad_part = nt(gp, w_in[...]).astype(bf16)
    part_own[...] = (tn(even, out_part[:n]) + tn(odd, grad_part[:n])).astype(bf16)
    part_other[...] = (tn(even, out_part[n:]) + tn(odd, grad_part[n:])).astype(bf16)
    both = jnp.concatenate([rows_in, rows_grad], axis=0)
    turned[...] = jnp.transpose(both.astype(f32)).astype(bf16)
    yh, j0 = place[0], place[1]
    depth = turned.shape[0] // 16
    for m, chunk in enumerate((c0, c1, c2, c3)):
        chunk[0 : 2 * n, :] = gp
        chunk[2 * n : 4 * n, :] = act
        j = jnp.bitwise_xor(j0, m)
        pieces = []
        for k in range(4):
            at = (lax.rem(yh + k, 4) * QUADS + j) * depth
            pieces.append(turned[pl.ds(pl.multiple_of(at, 16), depth), :])
        piece = jnp.concatenate(pieces, axis=0)
        for b in range(5):
            chunk[4 * n : 6 * n, 128 * b : 128 * (b + 1)] = piece[64 * b : 64 * (b + 1)]


def term_kernel(c0, c1, c2, c3, _, keep, s1, s2, s3):
    left, right = [], []
    zero = jnp.zeros((64, 640), bf16)
    for chunk in (c0, c1, c2, c3):
        left.append(jnp.concatenate([chunk[128:192, 128 * b : 128 * (b + 1)] for b in range(5)], axis=0))
        right.append(jnp.concatenate([chunk[0:64, :], zero], axis=1))
        right.append(jnp.concatenate([zero, chunk[64:128, :]], axis=1))
    total = nn(jnp.concatenate(left, axis=1), jnp.concatenate(right, axis=0))
    depth = keep.shape[0]
    keep[...] = total[:depth]
    for k, s in enumerate((s1, s2, s3)):
        s[...] = total[(k + 1) * depth : (k + 2) * depth].astype(bf16)


def finish_kernel(tok, cot, sp, parts, disp, comb, mixed, grad_tokens, done):
    done[...] = jnp.zeros_like(done)
    r = lax.broadcasted_iota(jnp.int32, (16, 2 * CHIP_COUNT), 0)
    c = lax.broadcasted_iota(jnp.int32, (16, 2 * CHIP_COUNT), 1)
    sel = jnp.where(((c % 2) * EXPERTS + c // (2 * SPREAD)) == r, 1.0, 0.0).astype(bf16)
    slots = nn(sel, parts[...])
    slot_out = slots[:8].astype(bf16)
    grad_slot_in = slots[8:].astype(bf16)
    d, cm = disp[...], comb[...]
    mixed[...] = tn(cm.astype(bf16), slot_out).astype(bf16)
    combine_grad = nt(slot_out, cot[...])
    dispatch_grad = nt(grad_slot_in, tok[...])
    lg = cm * (combine_grad - jnp.sum(cm * combine_grad, axis=0, keepdims=True))
    lg = lg + d * (dispatch_grad - jnp.sum(d * dispatch_grad, axis=1, keepdims=True))
    rows = jnp.concatenate([d.astype(bf16).astype(f32), lg.astype(bf16).astype(f32)], axis=0)
    cols = jnp.concatenate([grad_slot_in.astype(f32), sp[...].astype(f32)], axis=0)
    grad_tokens[...] = tn(rows.astype(bf16), cols.astype(bf16)).astype(bf16)


def total_kernel(keep, a, b, c, _, grad_in, grad_out):
    total = keep[...] + a[...].astype(f32) + b[...].astype(f32) + c[...].astype(f32)
    hidden = grad_in.shape[1]
    grad_in[...] = total[:, :hidden]
    grad_out[...] = total[:, hidden:]


def per_device(tokens, cotangent, slot_params, in_weight, out_weight):
    tok, cot = tokens[0], cotangent[0]
    patch, width = tok.shape
    hidden = in_weight.shape[1]
    sp = slot_params.T
    n2 = 2 * CHIP_COUNT
    send, disp, comb = call(
        route_kernel,
        [((n2, width), bf16), ((EXPERTS, patch), f32), ((EXPERTS, patch), f32)],
        10**7, 1500000, "hhv",
        [pltpu.VMEM((patch, width), bf16)] * 2 + [pltpu.SemaphoreType.DMA((2,))], 62_000_000,
    )(tok, cot, sp)

    def exchange(rows):
        got = lax.all_to_all(rows.reshape(CHIP_COUNT, 2, width), CHIPS, 0, 0, tiled=True)
        return got.reshape(n2, width)

    swap = [(0, 1), (1, 0)]
    own = exchange(send)
    other = lax.ppermute(own, "c", swap)
    place = jnp.stack([lax.axis_index("yh"), lax.axis_index(QUAD)]).astype(jnp.int32)
    chunk_shape = ((192, hidden), bf16)
    part_own, part_other, c0, c1, c2, c3 = call(
        expert_kernel,
        [((n2, width), bf16), ((n2, width), bf16)] + [chunk_shape] * 4,
        5 * 10**8, 4500000, "svvvv", [pltpu.VMEM((width, 128), bf16)],
    )(place, own, other, in_weight, out_weight)

    back = lax.ppermute(part_other, "c", swap)
    got = [c0]
    for m, chunk in ((1, c1), (2, c2), (3, c3)):
        got.append(lax.ppermute(chunk, QUAD, [(i, i ^ m) for i in range(QUADS)]))
    returned = (part_own.astype(f32) + back.astype(f32)).astype(bf16)
    parts = exchange(returned)

    depth = width // 16
    piece = ((depth, 2 * hidden), bf16)
    keep, s1, s2, s3 = call(
        term_kernel,
        [((depth, 2 * hidden), f32), piece, piece, piece],
        4 * 10**8, 2500000, "vvvva",
    )(*got, returned)
    shares = [
        lax.ppermute(s, "yh", [(i, (i + k) % 4) for i in range(4)]) for k, s in ((2, s2), (1, s1), (3, s3))
    ]

    mixed, grad_tokens, done = call(
        finish_kernel,
        [((patch, width), bf16), ((patch, width), bf16), ((8, 128), f32)],
        3 * 10**7, 3000000, "vvvvvv",
    )(tok, cot, sp, parts, disp, comb)
    grad_in, grad_out = call(
        total_kernel, [((depth, hidden), f32)] * 2, 10**6, 1500000, "vvvva",
    )(keep, *shares, done)
    return mixed[None], grad_tokens[None], grad_in, grad_out


def solution(mesh):
    fine = Mesh(np.asarray(mesh.devices).reshape(SIZES), AXES)
    return jax.shard_map(
        per_device,
        mesh=fine,
        in_specs=(P(AXES), P(AXES), P(), P(None, PEERS), P(None, PEERS)),
        out_specs=(P(AXES), P(AXES), P(DP, PEERS), P(DP, PEERS)),
        check_vma=False,
    )
```

```python
import functools

import jax
import jax.numpy as jnp
import numpy as np
from jax import lax
from jax.experimental import pallas as pl
from jax.experimental.pallas import tpu as pltpu
from jax.sharding import Mesh
from jax.sharding import PartitionSpec as P

root_half = 0.7071067811865476
density = 0.3989422804014327
f32 = jnp.float32
bf16 = jnp.bfloat16

AXES = ("yh", "yl", "xl", "xh", "zh", "zl", "c")
SIZES = (4, 2, 2, 2, 4, 4, 2)
DP = ("yh", "yl", "xl")
PEERS = ("xh", "zh", "zl", "c")
CHIPS = ("xh", "zh", "zl")
QUAD = ("yl", "xl")
EXPERTS, SPREAD, CHIP_COUNT = 8, 4, 32
QUADS = 4
PIECES = 4
ROOM = 20_000_000


def nn(a, b):
    return lax.dot_general(a, b, (((1,), (0,)), ((), ())), preferred_element_type=f32)


def nt(a, b):
    return lax.dot_general(a, b, (((1,), (1,)), ((), ())), preferred_element_type=f32)


def tn(a, b):
    return lax.dot_general(a, b, (((0,), (0,)), ((), ())), preferred_element_type=f32)


def pick(rows, cols, source):
    r = lax.broadcasted_iota(jnp.int32, (rows, cols), 0)
    c = lax.broadcasted_iota(jnp.int32, (rows, cols), 1)
    return jnp.where(c == source(r), 1.0, 0.0).astype(bf16)


def call(kernel, outs, flops, nbytes, ins, scratch=(), room=ROOM):
    vm = pl.BlockSpec(memory_space=pltpu.VMEM)
    spaces = {"v": vm, "s": pl.BlockSpec(memory_space=pltpu.SMEM), "a": pl.BlockSpec(memory_space=pl.ANY)}
    spaces["h"] = pl.BlockSpec(memory_space=pltpu.HBM)
    specs = [spaces[letter] for letter in ins]
    return pl.pallas_call(
        kernel,
        out_shape=[jax.ShapeDtypeStruct(s, d) for s, d in outs],
        in_specs=specs,
        out_specs=[vm] * len(outs),
        scratch_shapes=list(scratch),
        compiler_params=pltpu.CompilerParams(vmem_limit_bytes=room),
        cost_estimate=pl.CostEstimate(flops=flops, bytes_accessed=nbytes, transcendentals=0),
    )


def route_kernel(tok_hbm, cot_hbm, sp, send, disp, comb, tok, cot, sems):
    step = tok.shape[0] // PIECES
    copies = []
    for i, (src, dst) in enumerate(((tok_hbm, tok), (cot_hbm, cot))):
        for p in range(PIECES):
            rows = pl.ds(p * step, step)
            copies.append(pltpu.make_async_copy(src.at[rows], dst.at[rows], sems.at[i, p]))
            copies[-1].start()
    for copy in copies[:PIECES]:
        copy.wait()
    logits = nt(sp[...], tok[...])
    ed = jnp.exp(logits - jnp.max(logits, axis=1, keepdims=True))
    d = ed / jnp.sum(ed, axis=1, keepdims=True)
    ec = jnp.exp(logits - jnp.max(logits, axis=0, keepdims=True))
    c = ec / jnp.sum(ec, axis=0, keepdims=True)
    disp[...] = d
    comb[...] = c
    slot_in = nn(d.astype(bf16), tok[...]).astype(bf16)
    for copy in copies[PIECES:]:
        copy.wait()
    slot_grad = nn(c.astype(bf16), cot[...]).astype(bf16)
    both = jnp.concatenate([slot_in.astype(f32), slot_grad.astype(f32)], axis=0).astype(bf16)
    rows = 2 * CHIP_COUNT
    sel = pick(rows, 16, lambda r: (r % 2) * EXPERTS + r // (2 * SPREAD))
    send[...] = nn(sel, both).astype(bf16)


def expert_kernel(place, own, other, w_in, w_out, part_own, part_other, c0, c1, c2, c3, turned):
    n = own.shape[0] // 2
    even = pick(n, 2 * n, lambda r: 2 * r)
    odd = pick(n, 2 * n, lambda r: 2 * r + 1)
    rows_in = jnp.concatenate([nn(even, own[...]), nn(even, other[...])], axis=0).astype(bf16)
    rows_grad = jnp.concatenate([nn(odd, own[...]), nn(odd, other[...])], axis=0).astype(bf16)
    preact = nn(rows_in, w_in[...])
    hidden_grad = nn(rows_grad, w_out[...])
    cumulative = 0.5 * (1.0 + lax.erf(preact * root_half))
    slope = cumulative + preact * jnp.exp(-0.5 * preact * preact) * density
    act = (preact * cumulative).astype(bf16)
    gp = (hidden_grad * slope).astype(bf16)
    out_part = nt(act, w_out[...]).astype(bf16)
    grad_part = nt(gp, w_in[...]).astype(bf16)
    part_own[...] = (tn(even, out_part[:n]) + tn(odd, grad_part[:n])).astype(bf16)
    part_other[...] = (tn(even, out_part[n:]) + tn(odd, grad_part[n:])).astype(bf16)
    both = jnp.concatenate([rows_in, rows_grad], axis=0)
    turned[...] = jnp.transpose(both.astype(f32)).astype(bf16)
    j0 = place[0]
    depth = turned.shape[0] // 16
    for m, chunk in enumerate((c0, c1, c2, c3)):
        chunk[0 : 2 * n, :] = gp
        chunk[2 * n : 4 * n, :] = act
        j = jnp.bitwise_xor(j0, m)
        pieces = []
        for k in range(4):
            at = (k * QUADS + j) * depth
            pieces.append(turned[pl.ds(pl.multiple_of(at, 16), depth), :])
        piece = jnp.concatenate(pieces, axis=0)
        for b in range(5):
            chunk[4 * n : 6 * n, 128 * b : 128 * (b + 1)] = piece[64 * b : 64 * (b + 1)]


def term_kernel(c0, c1, c2, c3, _, terms):
    left, right = [], []
    zero = jnp.zeros((64, 640), bf16)
    for chunk in (c0, c1, c2, c3):
        left.append(jnp.concatenate([chunk[128:192, 128 * b : 128 * (b + 1)] for b in range(5)], axis=0))
        right.append(jnp.concatenate([chunk[0:64, :], zero], axis=1))
        right.append(jnp.concatenate([zero, chunk[64:128, :]], axis=1))
    total = nn(jnp.concatenate(left, axis=1), jnp.concatenate(right, axis=0))
    for k in range(terms.shape[0]):
        terms[k] = total[k * terms.shape[1] : (k + 1) * terms.shape[1]].astype(bf16)


def finish_kernel(tok, cot, sp, parts, disp, comb, mixed, grad_tokens, done):
    done[...] = jnp.zeros_like(done)
    r = lax.broadcasted_iota(jnp.int32, (16, 2 * CHIP_COUNT), 0)
    c = lax.broadcasted_iota(jnp.int32, (16, 2 * CHIP_COUNT), 1)
    sel = jnp.where(((c % 2) * EXPERTS + c // (2 * SPREAD)) == r, 1.0, 0.0).astype(bf16)
    slots = nn(sel, parts[...])
    slot_out = slots[:8].astype(bf16)
    grad_slot_in = slots[8:].astype(bf16)
    d, cm = disp[...], comb[...]
    mixed[...] = tn(cm.astype(bf16), slot_out).astype(bf16)
    combine_grad = nt(slot_out, cot[...])
    dispatch_grad = nt(grad_slot_in, tok[...])
    lg = cm * (combine_grad - jnp.sum(cm * combine_grad, axis=0, keepdims=True))
    lg = lg + d * (dispatch_grad - jnp.sum(d * dispatch_grad, axis=1, keepdims=True))
    rows = jnp.concatenate([d.astype(bf16).astype(f32), lg.astype(bf16).astype(f32)], axis=0)
    cols = jnp.concatenate([grad_slot_in.astype(f32), sp[...].astype(f32)], axis=0)
    grad_tokens[...] = tn(rows.astype(bf16), cols.astype(bf16)).astype(bf16)


def total_kernel(terms, _, grad_in, grad_out):
    total = terms[0].astype(f32)
    for k in range(1, terms.shape[0]):
        total = total + terms[k].astype(f32)
    hidden = grad_in.shape[1]
    grad_in[...] = total[:, :hidden]
    grad_out[...] = total[:, hidden:]


def per_device(tokens, cotangent, slot_params, in_weight, out_weight):
    tok, cot = tokens[0], cotangent[0]
    patch, width = tok.shape
    hidden = in_weight.shape[1]
    sp = slot_params.T
    n2 = 2 * CHIP_COUNT
    send, disp, comb = call(
        route_kernel,
        [((n2, width), bf16), ((EXPERTS, patch), f32), ((EXPERTS, patch), f32)],
        10**7, 1500000, "hhv",
        [pltpu.VMEM((patch, width), bf16)] * 2 + [pltpu.SemaphoreType.DMA((2, PIECES))], 56_000_000,
    )(tok, cot, sp)

    def exchange(rows):
        got = lax.all_to_all(rows.reshape(CHIP_COUNT, 2, width), CHIPS, 0, 0, tiled=True)
        return got.reshape(n2, width)

    swap = [(0, 1), (1, 0)]
    own = exchange(send)
    other = lax.ppermute(own, "c", swap)
    place = lax.axis_index(QUAD).astype(jnp.int32).reshape(1)
    chunk_shape = ((192, hidden), bf16)
    part_own, part_other, c0, c1, c2, c3 = call(
        expert_kernel,
        [((n2, width), bf16), ((n2, width), bf16)] + [chunk_shape] * 4,
        5 * 10**8, 4500000, "svvvv", [pltpu.VMEM((width, 128), bf16)],
    )(place, own, other, in_weight, out_weight)

    back = lax.ppermute(part_other, "c", swap)
    got = [c0]
    for m, chunk in ((1, c1), (2, c2), (3, c3)):
        got.append(lax.ppermute(chunk, QUAD, [(i, i ^ m) for i in range(QUADS)]))
    returned = (part_own.astype(f32) + back.astype(f32)).astype(bf16)
    parts = exchange(returned)

    depth = width // 16
    (terms,) = call(
        term_kernel, [((4, depth, 2 * hidden), bf16)], 4 * 10**8, 2500000, "vvvva",
    )(*got, returned)
    shares = lax.all_to_all(terms, "yh", 0, 0, tiled=True)

    mixed, grad_tokens, done = call(
        finish_kernel,
        [((patch, width), bf16), ((patch, width), bf16), ((8, 128), f32)],
        3 * 10**7, 3000000, "vvvvvv",
    )(tok, cot, sp, parts, disp, comb)
    grad_in, grad_out = call(
        total_kernel, [((depth, hidden), f32)] * 2, 10**6, 1500000, "va",
    )(shares, done)
    return mixed[None], grad_tokens[None], grad_in, grad_out


def solution(mesh):
    fine = Mesh(np.asarray(mesh.devices).reshape(SIZES), AXES)
    return jax.shard_map(
        per_device,
        mesh=fine,
        in_specs=(P(AXES), P(AXES), P(), P(None, PEERS), P(None, PEERS)),
        out_specs=(P(AXES), P(AXES), P(DP, PEERS), P(DP, PEERS)),
        check_vma=False,
    )
```

```python
import functools

import jax
import jax.numpy as jnp
import numpy as np
from jax import lax
from jax.experimental import pallas as pl
from jax.experimental.pallas import tpu as pltpu
from jax.sharding import Mesh
from jax.sharding import PartitionSpec as P

root_half = 0.7071067811865476
density = 0.3989422804014327
f32 = jnp.float32
bf16 = jnp.bfloat16

AXES = ("yh", "yl", "xl", "xh", "zh", "zl", "c")
SIZES = (4, 2, 2, 2, 4, 4, 2)
DP = ("yh", "yl", "xl")
PEERS = ("xh", "zh", "zl", "c")
CHIPS = ("xh", "zh", "zl")
QUAD = ("yl", "xl")
EXPERTS, SPREAD, CHIP_COUNT = 8, 4, 32
QUADS = 4
PIECES = 4
ROOM = 20_000_000


def nn(a, b):
    return lax.dot_general(a, b, (((1,), (0,)), ((), ())), preferred_element_type=f32)


def nt(a, b):
    return lax.dot_general(a, b, (((1,), (1,)), ((), ())), preferred_element_type=f32)


def tn(a, b):
    return lax.dot_general(a, b, (((0,), (0,)), ((), ())), preferred_element_type=f32)


def pick(rows, cols, source):
    r = lax.broadcasted_iota(jnp.int32, (rows, cols), 0)
    c = lax.broadcasted_iota(jnp.int32, (rows, cols), 1)
    return jnp.where(c == source(r), 1.0, 0.0).astype(bf16)


def call(kernel, outs, flops, nbytes, ins, scratch=(), room=ROOM):
    vm = pl.BlockSpec(memory_space=pltpu.VMEM)
    spaces = {"v": vm, "s": pl.BlockSpec(memory_space=pltpu.SMEM), "a": pl.BlockSpec(memory_space=pl.ANY)}
    spaces["h"] = pl.BlockSpec(memory_space=pltpu.HBM)
    specs = [spaces[letter] for letter in ins]
    return pl.pallas_call(
        kernel,
        out_shape=[jax.ShapeDtypeStruct(s, d) for s, d in outs],
        in_specs=specs,
        out_specs=[vm] * len(outs),
        scratch_shapes=list(scratch),
        compiler_params=pltpu.CompilerParams(vmem_limit_bytes=room),
        cost_estimate=pl.CostEstimate(flops=flops, bytes_accessed=nbytes, transcendentals=0),
    )


def route_kernel(tok_hbm, cot_hbm, sp, send, disp, comb, tok, cot, sems):
    step = tok.shape[0] // PIECES
    copies = []
    for i, (src, dst) in enumerate(((tok_hbm, tok), (cot_hbm, cot))):
        for p in range(PIECES):
            rows = pl.ds(p * step, step)
            copies.append(pltpu.make_async_copy(src.at[rows], dst.at[rows], sems.at[i, p]))
            copies[-1].start()
    for copy in copies[:PIECES]:
        copy.wait()
    logits = nt(sp[...], tok[...])
    ed = jnp.exp(logits - jnp.max(logits, axis=1, keepdims=True))
    d = ed / jnp.sum(ed, axis=1, keepdims=True)
    ec = jnp.exp(logits - jnp.max(logits, axis=0, keepdims=True))
    c = ec / jnp.sum(ec, axis=0, keepdims=True)
    disp[...] = d
    comb[...] = c
    slot_in = nn(d.astype(bf16), tok[...]).astype(bf16)
    for copy in copies[PIECES:]:
        copy.wait()
    slot_grad = nn(c.astype(bf16), cot[...]).astype(bf16)
    both = jnp.concatenate([slot_in.astype(f32), slot_grad.astype(f32)], axis=0).astype(bf16)
    rows = 2 * CHIP_COUNT
    sel = pick(rows, 16, lambda r: (r % 2) * EXPERTS + r // (2 * SPREAD))
    send[...] = nn(sel, both).astype(bf16)


def expert_kernel(place, own, other, w_in, w_out_hbm, part_own, part_other, c0, c1, c2, c3, turned, w_out, sems):
    step = w_out.shape[0] // PIECES
    copies = []
    for p in range(PIECES):
        rows = pl.ds(p * step, step)
        copies.append(pltpu.make_async_copy(w_out_hbm.at[rows], w_out.at[rows], sems.at[p]))
        copies[-1].start()
    n = own.shape[0] // 2
    even = pick(n, 2 * n, lambda r: 2 * r)
    odd = pick(n, 2 * n, lambda r: 2 * r + 1)
    rows_in = jnp.concatenate([nn(even, own[...]), nn(even, other[...])], axis=0).astype(bf16)
    rows_grad = jnp.concatenate([nn(odd, own[...]), nn(odd, other[...])], axis=0).astype(bf16)
    preact = nn(rows_in, w_in[...])
    for copy in copies:
        copy.wait()
    hidden_grad = nn(rows_grad, w_out[...])
    cumulative = 0.5 * (1.0 + lax.erf(preact * root_half))
    slope = cumulative + preact * jnp.exp(-0.5 * preact * preact) * density
    act = (preact * cumulative).astype(bf16)
    gp = (hidden_grad * slope).astype(bf16)
    out_part = nt(act, w_out[...]).astype(bf16)
    grad_part = nt(gp, w_in[...]).astype(bf16)
    part_own[...] = (tn(even, out_part[:n]) + tn(odd, grad_part[:n])).astype(bf16)
    part_other[...] = (tn(even, out_part[n:]) + tn(odd, grad_part[n:])).astype(bf16)
    both = jnp.concatenate([rows_in, rows_grad], axis=0)
    turned[...] = jnp.transpose(both.astype(f32)).astype(bf16)
    yh, j0 = place[0], place[1]
    depth = turned.shape[0] // 16
    for m, chunk in enumerate((c0, c1, c2, c3)):
        chunk[0 : 2 * n, :] = gp
        chunk[2 * n : 4 * n, :] = act
        j = jnp.bitwise_xor(j0, m)
        pieces = []
        for k in range(4):
            at = (lax.rem(yh + k, 4) * QUADS + j) * depth
            pieces.append(turned[pl.ds(pl.multiple_of(at, 16), depth), :])
        piece = jnp.concatenate(pieces, axis=0)
        for b in range(5):
            chunk[4 * n : 6 * n, 128 * b : 128 * (b + 1)] = piece[64 * b : 64 * (b + 1)]


def term_kernel(c0, c1, c2, c3, _, keep, s1, s2, s3):
    left, right = [], []
    zero = jnp.zeros((64, 640), bf16)
    for chunk in (c0, c1, c2, c3):
        left.append(jnp.concatenate([chunk[128:192, 128 * b : 128 * (b + 1)] for b in range(5)], axis=0))
        right.append(jnp.concatenate([chunk[0:64, :], zero], axis=1))
        right.append(jnp.concatenate([zero, chunk[64:128, :]], axis=1))
    total = nn(jnp.concatenate(left, axis=1), jnp.concatenate(right, axis=0))
    depth = keep.shape[0]
    keep[...] = total[:depth]
    for k, s in enumerate((s1, s2, s3)):
        s[...] = total[(k + 1) * depth : (k + 2) * depth].astype(bf16)


def finish_kernel(tok, cot, sp, parts, disp, comb, mixed, grad_tokens, done):
    done[...] = jnp.zeros_like(done)
    r = lax.broadcasted_iota(jnp.int32, (16, 2 * CHIP_COUNT), 0)
    c = lax.broadcasted_iota(jnp.int32, (16, 2 * CHIP_COUNT), 1)
    sel = jnp.where(((c % 2) * EXPERTS + c // (2 * SPREAD)) == r, 1.0, 0.0).astype(bf16)
    slots = nn(sel, parts[...])
    slot_out = slots[:8].astype(bf16)
    grad_slot_in = slots[8:].astype(bf16)
    d, cm = disp[...], comb[...]
    mixed[...] = tn(cm.astype(bf16), slot_out).astype(bf16)
    combine_grad = nt(slot_out, cot[...])
    dispatch_grad = nt(grad_slot_in, tok[...])
    lg = cm * (combine_grad - jnp.sum(cm * combine_grad, axis=0, keepdims=True))
    lg = lg + d * (dispatch_grad - jnp.sum(d * dispatch_grad, axis=1, keepdims=True))
    rows = jnp.concatenate([d.astype(bf16).astype(f32), lg.astype(bf16).astype(f32)], axis=0)
    cols = jnp.concatenate([grad_slot_in.astype(f32), sp[...].astype(f32)], axis=0)
    grad_tokens[...] = tn(rows.astype(bf16), cols.astype(bf16)).astype(bf16)


def total_kernel(keep, a, b, c, _, grad_in, grad_out):
    total = keep[...] + a[...].astype(f32) + b[...].astype(f32) + c[...].astype(f32)
    hidden = grad_in.shape[1]
    grad_in[...] = total[:, :hidden]
    grad_out[...] = total[:, hidden:]


def per_device(tokens, cotangent, slot_params, in_weight, out_weight):
    tok, cot = tokens[0], cotangent[0]
    patch, width = tok.shape
    hidden = in_weight.shape[1]
    sp = slot_params.T
    n2 = 2 * CHIP_COUNT
    send, disp, comb = call(
        route_kernel,
        [((n2, width), bf16), ((EXPERTS, patch), f32), ((EXPERTS, patch), f32)],
        10**7, 1500000, "hhv",
        [pltpu.VMEM((patch, width), bf16)] * 2 + [pltpu.SemaphoreType.DMA((2, PIECES))], 56_000_000,
    )(tok, cot, sp)

    def exchange(rows):
        got = lax.all_to_all(rows.reshape(CHIP_COUNT, 2, width), CHIPS, 0, 0, tiled=True)
        return got.reshape(n2, width)

    swap = [(0, 1), (1, 0)]
    own = exchange(send)
    other = lax.ppermute(own, "c", swap)
    place = jnp.stack([lax.axis_index("yh"), lax.axis_index(QUAD)]).astype(jnp.int32)
    chunk_shape = ((192, hidden), bf16)
    part_own, part_other, c0, c1, c2, c3 = call(
        expert_kernel,
        [((n2, width), bf16), ((n2, width), bf16)] + [chunk_shape] * 4,
        5 * 10**8, 4500000, "svvvh",
        [pltpu.VMEM((width, 128), bf16), pltpu.VMEM((width, hidden), bf16), pltpu.SemaphoreType.DMA((PIECES,))],
        53_000_000,
    )(place, own, other, in_weight, out_weight)

    back = lax.ppermute(part_other, "c", swap)
    got = [c0]
    for m, chunk in ((1, c1), (2, c2), (3, c3)):
        got.append(lax.ppermute(chunk, QUAD, [(i, i ^ m) for i in range(QUADS)]))
    returned = (part_own.astype(f32) + back.astype(f32)).astype(bf16)
    parts = exchange(returned)

    depth = width // 16
    piece = ((depth, 2 * hidden), bf16)
    keep, s1, s2, s3 = call(
        term_kernel,
        [((depth, 2 * hidden), f32), piece, piece, piece],
        12 * 10**9, 2500000, "vvvva",
    )(*got, returned)
    shares = [
        lax.ppermute(s, "yh", [(i, (i + k) % 4) for i in range(4)]) for k, s in ((2, s2), (1, s1), (3, s3))
    ]

    mixed, grad_tokens, done = call(
        finish_kernel,
        [((patch, width), bf16), ((patch, width), bf16), ((8, 128), f32)],
        3 * 10**7, 3000000, "vvvvvv",
    )(tok, cot, sp, parts, disp, comb)
    grad_in, grad_out = call(
        total_kernel, [((depth, hidden), f32)] * 2, 10**6, 1500000, "vvvva",
    )(keep, *shares, done)
    return mixed[None], grad_tokens[None], grad_in, grad_out


def solution(mesh):
    fine = Mesh(np.asarray(mesh.devices).reshape(SIZES), AXES)
    return jax.shard_map(
        per_device,
        mesh=fine,
        in_specs=(P(AXES), P(AXES), P(), P(None, PEERS), P(None, PEERS)),
        out_specs=(P(AXES), P(AXES), P(DP, PEERS), P(DP, PEERS)),
        check_vma=False,
    )
```

```python
import functools

import jax
import jax.numpy as jnp
import numpy as np
from jax import lax
from jax.experimental import pallas as pl
from jax.experimental.pallas import tpu as pltpu
from jax.sharding import Mesh
from jax.sharding import PartitionSpec as P

root_half = 0.7071067811865476
density = 0.3989422804014327
f32 = jnp.float32
bf16 = jnp.bfloat16

AXES = ("yh", "yl", "xl", "xh", "zh", "zl", "c")
SIZES = (4, 2, 2, 2, 4, 4, 2)
DP = ("yh", "yl", "xl")
PEERS = ("xh", "zh", "zl", "c")
CHIPS = ("xh", "zh", "zl")
QUAD = ("yl", "xl")
EXPERTS, SPREAD, CHIP_COUNT = 8, 4, 32
QUADS = 4
PIECES = 4
ROOM = 20_000_000


def nn(a, b):
    return lax.dot_general(a, b, (((1,), (0,)), ((), ())), preferred_element_type=f32)


def nt(a, b):
    return lax.dot_general(a, b, (((1,), (1,)), ((), ())), preferred_element_type=f32)


def tn(a, b):
    return lax.dot_general(a, b, (((0,), (0,)), ((), ())), preferred_element_type=f32)


def pick(rows, cols, source):
    r = lax.broadcasted_iota(jnp.int32, (rows, cols), 0)
    c = lax.broadcasted_iota(jnp.int32, (rows, cols), 1)
    return jnp.where(c == source(r), 1.0, 0.0).astype(bf16)


def call(kernel, outs, flops, nbytes, ins, scratch=(), room=ROOM):
    vm = pl.BlockSpec(memory_space=pltpu.VMEM)
    spaces = {"v": vm, "s": pl.BlockSpec(memory_space=pltpu.SMEM), "a": pl.BlockSpec(memory_space=pl.ANY)}
    spaces["h"] = pl.BlockSpec(memory_space=pltpu.HBM)
    specs = [spaces[letter] for letter in ins]
    return pl.pallas_call(
        kernel,
        out_shape=[jax.ShapeDtypeStruct(s, d) for s, d in outs],
        in_specs=specs,
        out_specs=[vm] * len(outs),
        scratch_shapes=list(scratch),
        compiler_params=pltpu.CompilerParams(vmem_limit_bytes=room),
        cost_estimate=pl.CostEstimate(flops=flops, bytes_accessed=nbytes, transcendentals=0),
    )


def start_pieces(pairs, sems):
    copies = []
    for i, (src, dst) in enumerate(pairs):
        step = dst.shape[0] // PIECES
        for p in range(PIECES):
            rows = pl.ds(p * step, step)
            copies.append(pltpu.make_async_copy(src.at[rows], dst.at[rows], sems.at[i, p]))
            copies[-1].start()
    return copies


def route_kernel(tok_hbm, cot_hbm, sp, send, disp, comb, tok, cot, sems):
    copies = start_pieces(((tok_hbm, tok), (cot_hbm, cot)), sems)
    for copy in copies[:PIECES]:
        copy.wait()
    logits = nt(sp[...], tok[...])
    ed = jnp.exp(logits - jnp.max(logits, axis=1, keepdims=True))
    d = ed / jnp.sum(ed, axis=1, keepdims=True)
    ec = jnp.exp(logits - jnp.max(logits, axis=0, keepdims=True))
    c = ec / jnp.sum(ec, axis=0, keepdims=True)
    disp[...] = d
    comb[...] = c
    slot_in = nn(d.astype(bf16), tok[...]).astype(bf16)
    for copy in copies[PIECES:]:
        copy.wait()
    slot_grad = nn(c.astype(bf16), cot[...]).astype(bf16)
    both = jnp.concatenate([slot_in.astype(f32), slot_grad.astype(f32)], axis=0).astype(bf16)
    rows = 2 * CHIP_COUNT
    sel = pick(rows, 16, lambda r: (r % 2) * EXPERTS + r // (2 * SPREAD))
    send[...] = nn(sel, both).astype(bf16)


def expert_kernel(place, own, other, w_in, w_out_hbm, part_own, part_other, c0, c1, c2, c3, turned, w_out, sems):
    copies = start_pieces(((w_out_hbm, w_out),), sems)
    n = own.shape[0] // 2
    even = pick(n, 2 * n, lambda r: 2 * r)
    odd = pick(n, 2 * n, lambda r: 2 * r + 1)
    rows_in = jnp.concatenate([nn(even, own[...]), nn(even, other[...])], axis=0).astype(bf16)
    rows_grad = jnp.concatenate([nn(odd, own[...]), nn(odd, other[...])], axis=0).astype(bf16)
    preact = nn(rows_in, w_in[...])
    both = jnp.concatenate([rows_in, rows_grad], axis=0)
    turned[...] = jnp.transpose(both.astype(f32)).astype(bf16)
    yh, j0 = place[0], place[1]
    depth = turned.shape[0] // 16
    chunks = (c0, c1, c2, c3)
    for m, chunk in enumerate(chunks):
        j = jnp.bitwise_xor(j0, m)
        pieces = []
        for k in range(4):
            at = (lax.rem(yh + k, 4) * QUADS + j) * depth
            pieces.append(turned[pl.ds(pl.multiple_of(at, 16), depth), :])
        piece = jnp.concatenate(pieces, axis=0)
        for b in range(5):
            chunk[4 * n : 6 * n, 128 * b : 128 * (b + 1)] = piece[64 * b : 64 * (b + 1)]
    cumulative = 0.5 * (1.0 + lax.erf(preact * root_half))
    slope = cumulative + preact * jnp.exp(-0.5 * preact * preact) * density
    act = (preact * cumulative).astype(bf16)
    for chunk in chunks:
        chunk[2 * n : 4 * n, :] = act
    for copy in copies:
        copy.wait()
    hidden_grad = nn(rows_grad, w_out[...])
    gp = (hidden_grad * slope).astype(bf16)
    for chunk in chunks:
        chunk[0 : 2 * n, :] = gp
    out_part = nt(act, w_out[...]).astype(bf16)
    grad_part = nt(gp, w_in[...]).astype(bf16)
    part_own[...] = (tn(even, out_part[:n]) + tn(odd, grad_part[:n])).astype(bf16)
    part_other[...] = (tn(even, out_part[n:]) + tn(odd, grad_part[n:])).astype(bf16)


def term_kernel(c0, c1, c2, c3, _, keep, s1, s2, s3):
    left, right = [], []
    zero = jnp.zeros((64, 640), bf16)
    for chunk in (c0, c1, c2, c3):
        left.append(jnp.concatenate([chunk[128:192, 128 * b : 128 * (b + 1)] for b in range(5)], axis=0))
        right.append(jnp.concatenate([chunk[0:64, :], zero], axis=1))
        right.append(jnp.concatenate([zero, chunk[64:128, :]], axis=1))
    total = nn(jnp.concatenate(left, axis=1), jnp.concatenate(right, axis=0))
    depth = keep.shape[0]
    keep[...] = total[:depth]
    for k, s in enumerate((s1, s2, s3)):
        s[...] = total[(k + 1) * depth : (k + 2) * depth].astype(bf16)


def finish_kernel(tok_hbm, cot_hbm, sp, parts, disp, comb, mixed, grad_tokens, done, tok, cot, sems):
    copies = start_pieces(((tok_hbm, tok), (cot_hbm, cot)), sems)
    for copy in copies:
        copy.wait()
    done[...] = jnp.zeros_like(done)
    r = lax.broadcasted_iota(jnp.int32, (16, 2 * CHIP_COUNT), 0)
    c = lax.broadcasted_iota(jnp.int32, (16, 2 * CHIP_COUNT), 1)
    sel = jnp.where(((c % 2) * EXPERTS + c // (2 * SPREAD)) == r, 1.0, 0.0).astype(bf16)
    slots = nn(sel, parts[...])
    slot_out = slots[:8].astype(bf16)
    grad_slot_in = slots[8:].astype(bf16)
    d, cm = disp[...], comb[...]
    mixed[...] = tn(cm.astype(bf16), slot_out).astype(bf16)
    combine_grad = nt(slot_out, cot[...])
    dispatch_grad = nt(grad_slot_in, tok[...])
    lg = cm * (combine_grad - jnp.sum(cm * combine_grad, axis=0, keepdims=True))
    lg = lg + d * (dispatch_grad - jnp.sum(d * dispatch_grad, axis=1, keepdims=True))
    rows = jnp.concatenate([d.astype(bf16).astype(f32), lg.astype(bf16).astype(f32)], axis=0)
    cols = jnp.concatenate([grad_slot_in.astype(f32), sp[...].astype(f32)], axis=0)
    grad_tokens[...] = tn(rows.astype(bf16), cols.astype(bf16)).astype(bf16)


def total_kernel(keep, a, b, c, _, grad_in, grad_out):
    total = keep[...] + a[...].astype(f32) + b[...].astype(f32) + c[...].astype(f32)
    hidden = grad_in.shape[1]
    grad_in[...] = total[:, :hidden]
    grad_out[...] = total[:, hidden:]


def per_device(tokens, cotangent, slot_params, in_weight, out_weight):
    tok, cot = tokens[0], cotangent[0]
    patch, width = tok.shape
    hidden = in_weight.shape[1]
    sp = slot_params.T
    n2 = 2 * CHIP_COUNT
    send, disp, comb = call(
        route_kernel,
        [((n2, width), bf16), ((EXPERTS, patch), f32), ((EXPERTS, patch), f32)],
        10**7, 1500000, "hhv",
        [pltpu.VMEM((patch, width), bf16)] * 2 + [pltpu.SemaphoreType.DMA((2, PIECES))], 56_000_000,
    )(tok, cot, sp)

    def exchange(rows):
        got = lax.all_to_all(rows.reshape(CHIP_COUNT, 2, width), CHIPS, 0, 0, tiled=True)
        return got.reshape(n2, width)

    swap = [(0, 1), (1, 0)]
    own = exchange(send)
    other = lax.ppermute(own, "c", swap)
    place = jnp.stack([lax.axis_index("yh"), lax.axis_index(QUAD)]).astype(jnp.int32)
    chunk_shape = ((192, hidden), bf16)
    part_own, part_other, c0, c1, c2, c3 = call(
        expert_kernel,
        [((n2, width), bf16), ((n2, width), bf16)] + [chunk_shape] * 4,
        5 * 10**8, 4500000, "svvvh",
        [pltpu.VMEM((width, 128), bf16), pltpu.VMEM((width, hidden), bf16), pltpu.SemaphoreType.DMA((1, PIECES))],
        53_000_000,
    )(place, own, other, in_weight, out_weight)

    back = lax.ppermute(part_other, "c", swap)
    got = [c0]
    for m, chunk in ((1, c1), (2, c2), (3, c3)):
        got.append(lax.ppermute(chunk, QUAD, [(i, i ^ m) for i in range(QUADS)]))
    returned = (part_own.astype(f32) + back.astype(f32)).astype(bf16)
    parts = exchange(returned)

    depth = width // 16
    piece = ((depth, 2 * hidden), bf16)
    keep, s1, s2, s3 = call(
        term_kernel,
        [((depth, 2 * hidden), f32), piece, piece, piece],
        12 * 10**9, 2500000, "vvvva",
    )(*got, returned)
    shares = [
        lax.ppermute(s, "yh", [(i, (i + k) % 4) for i in range(4)]) for k, s in ((2, s2), (1, s1), (3, s3))
    ]

    mixed, grad_tokens, done = call(
        finish_kernel,
        [((patch, width), bf16), ((patch, width), bf16), ((8, 128), f32)],
        3 * 10**7, 3000000, "hhvvvv",
        [pltpu.VMEM((patch, width), bf16)] * 2 + [pltpu.SemaphoreType.DMA((2, PIECES))], 56_000_000,
    )(tok, cot, sp, parts, disp, comb)
    grad_in, grad_out = call(
        total_kernel, [((depth, hidden), f32)] * 2, 10**6, 1500000, "vvvva",
    )(keep, *shares, done)
    return mixed[None], grad_tokens[None], grad_in, grad_out


def solution(mesh):
    fine = Mesh(np.asarray(mesh.devices).reshape(SIZES), AXES)
    return jax.shard_map(
        per_device,
        mesh=fine,
        in_specs=(P(AXES), P(AXES), P(), P(None, PEERS), P(None, PEERS)),
        out_specs=(P(AXES), P(AXES), P(DP, PEERS), P(DP, PEERS)),
        check_vma=False,
    )
```

```python
import functools

import jax
import jax.numpy as jnp
import numpy as np
from jax import lax
from jax.experimental import pallas as pl
from jax.experimental.pallas import tpu as pltpu
from jax.sharding import Mesh
from jax.sharding import PartitionSpec as P

root_half = 0.7071067811865476
density = 0.3989422804014327
f32 = jnp.float32
bf16 = jnp.bfloat16

AXES = ("yh", "yl", "xl", "xh", "zh", "zl", "c")
SIZES = (4, 2, 2, 2, 4, 4, 2)
DP = ("yh", "yl", "xl")
PEERS = ("xh", "zh", "zl", "c")
CHIPS = ("xh", "zh", "zl")
QUAD = ("yl", "xl")
EXPERTS, SPREAD, CHIP_COUNT = 8, 4, 32
QUADS = 4
PIECES = 4
ROOM = 20_000_000


def nn(a, b):
    return lax.dot_general(a, b, (((1,), (0,)), ((), ())), preferred_element_type=f32)


def nt(a, b):
    return lax.dot_general(a, b, (((1,), (1,)), ((), ())), preferred_element_type=f32)


def tn(a, b):
    return lax.dot_general(a, b, (((0,), (0,)), ((), ())), preferred_element_type=f32)


def pick(rows, cols, source):
    r = lax.broadcasted_iota(jnp.int32, (rows, cols), 0)
    c = lax.broadcasted_iota(jnp.int32, (rows, cols), 1)
    return jnp.where(c == source(r), 1.0, 0.0).astype(bf16)


def call(kernel, outs, flops, nbytes, ins, scratch=(), room=ROOM):
    vm = pl.BlockSpec(memory_space=pltpu.VMEM)
    spaces = {"v": vm, "s": pl.BlockSpec(memory_space=pltpu.SMEM), "a": pl.BlockSpec(memory_space=pl.ANY)}
    spaces["h"] = pl.BlockSpec(memory_space=pltpu.HBM)
    specs = [spaces[letter] for letter in ins]
    return pl.pallas_call(
        kernel,
        out_shape=[jax.ShapeDtypeStruct(s, d) for s, d in outs],
        in_specs=specs,
        out_specs=[vm] * len(outs),
        scratch_shapes=list(scratch),
        compiler_params=pltpu.CompilerParams(vmem_limit_bytes=room),
        cost_estimate=pl.CostEstimate(flops=flops, bytes_accessed=nbytes, transcendentals=0),
    )


def start_pieces(pairs, sems):
    copies = []
    for i, (src, dst) in enumerate(pairs):
        step = dst.shape[0] // PIECES
        for p in range(PIECES):
            rows = pl.ds(p * step, step)
            copies.append(pltpu.make_async_copy(src.at[rows], dst.at[rows], sems.at[i, p]))
            copies[-1].start()
    return copies


def route_kernel(tok_hbm, cot_hbm, sp, send, disp, comb, tok, cot, sems):
    copies = start_pieces(((tok_hbm, tok), (cot_hbm, cot)), sems)
    for copy in copies[:PIECES]:
        copy.wait()
    logits = nt(sp[...], tok[...])
    ed = jnp.exp(logits - jnp.max(logits, axis=1, keepdims=True))
    d = ed / jnp.sum(ed, axis=1, keepdims=True)
    ec = jnp.exp(logits - jnp.max(logits, axis=0, keepdims=True))
    c = ec / jnp.sum(ec, axis=0, keepdims=True)
    disp[...] = d
    comb[...] = c
    slot_in = nn(d.astype(bf16), tok[...]).astype(bf16)
    for copy in copies[PIECES:]:
        copy.wait()
    slot_grad = nn(c.astype(bf16), cot[...]).astype(bf16)
    both = jnp.concatenate([slot_in.astype(f32), slot_grad.astype(f32)], axis=0).astype(bf16)
    rows = 2 * CHIP_COUNT
    sel = pick(rows, 16, lambda r: (r % 2) * EXPERTS + r // (2 * SPREAD))
    send[...] = nn(sel, both).astype(bf16)


def expert_kernel(place, own, other, w_in, w_out, part_own, part_other, c0, c1, c2, c3, turned):
    n = own.shape[0] // 2
    even = pick(n, 2 * n, lambda r: 2 * r)
    odd = pick(n, 2 * n, lambda r: 2 * r + 1)
    rows_in = jnp.concatenate([nn(even, own[...]), nn(even, other[...])], axis=0).astype(bf16)
    rows_grad = jnp.concatenate([nn(odd, own[...]), nn(odd, other[...])], axis=0).astype(bf16)
    preact = nn(rows_in, w_in[...])
    hidden_grad = nn(rows_grad, w_out[...])
    cumulative = 0.5 * (1.0 + lax.erf(preact * root_half))
    slope = cumulative + preact * jnp.exp(-0.5 * preact * preact) * density
    act = (preact * cumulative).astype(bf16)
    gp = (hidden_grad * slope).astype(bf16)
    out_part = nt(act, w_out[...]).astype(bf16)
    grad_part = nt(gp, w_in[...]).astype(bf16)
    part_own[...] = (tn(even, out_part[:n]) + tn(odd, grad_part[:n])).astype(bf16)
    part_other[...] = (tn(even, out_part[n:]) + tn(odd, grad_part[n:])).astype(bf16)
    both = jnp.concatenate([rows_in, rows_grad], axis=0)
    turned[...] = jnp.transpose(both.astype(f32)).astype(bf16)
    yh, j0 = place[0], place[1]
    depth = turned.shape[0] // 16
    for m, chunk in enumerate((c0, c1, c2, c3)):
        chunk[0 : 2 * n, :] = gp
        chunk[2 * n : 4 * n, :] = act
        j = jnp.bitwise_xor(j0, m)
        pieces = []
        for k in range(4):
            at = (lax.rem(yh + k, 4) * QUADS + j) * depth
            pieces.append(turned[pl.ds(pl.multiple_of(at, 16), depth), :])
        piece = jnp.concatenate(pieces, axis=0)
        for b in range(5):
            chunk[4 * n : 6 * n, 128 * b : 128 * (b + 1)] = piece[64 * b : 64 * (b + 1)]


def term_kernel(c0, c1, c2, c3, _, keep, s1, s2, s3):
    left, right = [], []
    zero = jnp.zeros((64, 640), bf16)
    for chunk in (c0, c1, c2, c3):
        left.append(jnp.concatenate([chunk[128:192, 128 * b : 128 * (b + 1)] for b in range(5)], axis=0))
        right.append(jnp.concatenate([chunk[0:64, :], zero], axis=1))
        right.append(jnp.concatenate([zero, chunk[64:128, :]], axis=1))
    total = nn(jnp.concatenate(left, axis=1), jnp.concatenate(right, axis=0))
    depth = keep.shape[0]
    keep[...] = total[:depth]
    for k, s in enumerate((s1, s2, s3)):
        s[...] = total[(k + 1) * depth : (k + 2) * depth].astype(bf16)


def finish_kernel(tok_hbm, cot_hbm, sp, parts, disp, comb, mixed, grad_tokens, done, tok, cot, sems):
    copies = start_pieces(((tok_hbm, tok), (cot_hbm, cot)), sems)
    for copy in copies:
        copy.wait()
    done[...] = jnp.zeros_like(done)
    r = lax.broadcasted_iota(jnp.int32, (16, 2 * CHIP_COUNT), 0)
    c = lax.broadcasted_iota(jnp.int32, (16, 2 * CHIP_COUNT), 1)
    sel = jnp.where(((c % 2) * EXPERTS + c // (2 * SPREAD)) == r, 1.0, 0.0).astype(bf16)
    slots = nn(sel, parts[...])
    slot_out = slots[:8].astype(bf16)
    grad_slot_in = slots[8:].astype(bf16)
    d, cm = disp[...], comb[...]
    mixed[...] = tn(cm.astype(bf16), slot_out).astype(bf16)
    combine_grad = nt(slot_out, cot[...])
    dispatch_grad = nt(grad_slot_in, tok[...])
    lg = cm * (combine_grad - jnp.sum(cm * combine_grad, axis=0, keepdims=True))
    lg = lg + d * (dispatch_grad - jnp.sum(d * dispatch_grad, axis=1, keepdims=True))
    rows = jnp.concatenate([d.astype(bf16).astype(f32), lg.astype(bf16).astype(f32)], axis=0)
    cols = jnp.concatenate([grad_slot_in.astype(f32), sp[...].astype(f32)], axis=0)
    grad_tokens[...] = tn(rows.astype(bf16), cols.astype(bf16)).astype(bf16)


def total_kernel(keep, a, b, c, _, grad_in, grad_out):
    total = keep[...] + a[...].astype(f32) + b[...].astype(f32) + c[...].astype(f32)
    hidden = grad_in.shape[1]
    grad_in[...] = total[:, :hidden]
    grad_out[...] = total[:, hidden:]


def per_device(tokens, cotangent, slot_params, in_weight, out_weight):
    tok, cot = tokens[0], cotangent[0]
    patch, width = tok.shape
    hidden = in_weight.shape[1]
    sp = slot_params.T
    n2 = 2 * CHIP_COUNT
    send, disp, comb = call(
        route_kernel,
        [((n2, width), bf16), ((EXPERTS, patch), f32), ((EXPERTS, patch), f32)],
        10**7, 1500000, "hhv",
        [pltpu.VMEM((patch, width), bf16)] * 2 + [pltpu.SemaphoreType.DMA((2, PIECES))],
        56_000_000,
    )(tok, cot, sp)

    def exchange(rows):
        got = lax.all_to_all(rows.reshape(CHIP_COUNT, 2, width), CHIPS, 0, 0, tiled=True)
        return got.reshape(n2, width)

    swap = [(0, 1), (1, 0)]
    own = exchange(send)
    other = lax.ppermute(own, "c", swap)
    place = jnp.stack([lax.axis_index("yh"), lax.axis_index(QUAD)]).astype(jnp.int32)
    chunk_shape = ((192, hidden), bf16)
    part_own, part_other, c0, c1, c2, c3 = call(
        expert_kernel,
        [((n2, width), bf16), ((n2, width), bf16)] + [chunk_shape] * 4,
        5 * 10**8, 4500000, "svvvv", [pltpu.VMEM((width, 128), bf16)],
    )(place, own, other, in_weight, out_weight)

    back = lax.ppermute(part_other, "c", swap)
    got = [c0]
    for m, chunk in ((3, c3), (1, c1), (2, c2)):
        got.append(lax.ppermute(chunk, QUAD, [(i, i ^ m) for i in range(QUADS)]))
    returned = (part_own.astype(f32) + back.astype(f32)).astype(bf16)
    parts = exchange(returned)

    depth = width // 16
    piece = ((depth, 2 * hidden), bf16)
    keep, s1, s2, s3 = call(
        term_kernel,
        [((depth, 2 * hidden), f32), piece, piece, piece],
        12 * 10**9, 2500000, "vvvva",
    )(*got, returned)
    shares = [
        lax.ppermute(s, "yh", [(i, (i + k) % 4) for i in range(4)]) for k, s in ((2, s2), (1, s1), (3, s3))
    ]

    mixed, grad_tokens, done = call(
        finish_kernel,
        [((patch, width), bf16), ((patch, width), bf16), ((8, 128), f32)],
        3 * 10**7, 3000000, "hhvvvv",
        [pltpu.VMEM((patch, width), bf16)] * 2 + [pltpu.SemaphoreType.DMA((2, PIECES))], 56_000_000,
    )(tok, cot, sp, parts, disp, comb)
    grad_in, grad_out = call(
        total_kernel, [((depth, hidden), f32)] * 2, 10**6, 1500000, "vvvva",
    )(keep, *shares, done)
    return mixed[None], grad_tokens[None], grad_in, grad_out


def solution(mesh):
    fine = Mesh(np.asarray(mesh.devices).reshape(SIZES), AXES)
    return jax.shard_map(
        per_device,
        mesh=fine,
        in_specs=(P(AXES), P(AXES), P(), P(None, PEERS), P(None, PEERS)),
        out_specs=(P(AXES), P(AXES), P(DP, PEERS), P(DP, PEERS)),
        check_vma=False,
    )
```

```python
import functools

import jax
import jax.numpy as jnp
import numpy as np
from jax import lax
from jax.experimental import pallas as pl
from jax.experimental.pallas import tpu as pltpu
from jax.sharding import Mesh
from jax.sharding import PartitionSpec as P

root_half = 0.7071067811865476
density = 0.3989422804014327
f32 = jnp.float32
bf16 = jnp.bfloat16

AXES = ("ya", "yb", "xl", "xh", "zh", "zl", "c")
SIZES = (2, 4, 2, 2, 4, 4, 2)
DP = ("ya", "yb", "xl")
Y, ROWS = ("ya", "yb"), 8
STEPS = (0, 2, 1, 7)
PEERS = ("xh", "zh", "zl", "c")
CHIPS = ("xh", "zh", "zl")
QUAD = ("ya", "xl")
EXPERTS, SPREAD, CHIP_COUNT = 8, 4, 32
QUADS = 4
PIECES = 4
ROOM = 20_000_000


def nn(a, b):
    return lax.dot_general(a, b, (((1,), (0,)), ((), ())), preferred_element_type=f32)


def nt(a, b):
    return lax.dot_general(a, b, (((1,), (1,)), ((), ())), preferred_element_type=f32)


def tn(a, b):
    return lax.dot_general(a, b, (((0,), (0,)), ((), ())), preferred_element_type=f32)


def pick(rows, cols, source):
    r = lax.broadcasted_iota(jnp.int32, (rows, cols), 0)
    c = lax.broadcasted_iota(jnp.int32, (rows, cols), 1)
    return jnp.where(c == source(r), 1.0, 0.0).astype(bf16)


def call(kernel, outs, flops, nbytes, ins, scratch=(), room=ROOM):
    vm = pl.BlockSpec(memory_space=pltpu.VMEM)
    spaces = {"v": vm, "s": pl.BlockSpec(memory_space=pltpu.SMEM), "a": pl.BlockSpec(memory_space=pl.ANY)}
    spaces["h"] = pl.BlockSpec(memory_space=pltpu.HBM)
    specs = [spaces[letter] for letter in ins]
    return pl.pallas_call(
        kernel,
        out_shape=[jax.ShapeDtypeStruct(s, d) for s, d in outs],
        in_specs=specs,
        out_specs=[vm] * len(outs),
        scratch_shapes=list(scratch),
        compiler_params=pltpu.CompilerParams(vmem_limit_bytes=room),
        cost_estimate=pl.CostEstimate(flops=flops, bytes_accessed=nbytes, transcendentals=0),
    )


def start_pieces(pairs, sems):
    copies = []
    for i, (src, dst) in enumerate(pairs):
        step = dst.shape[0] // PIECES
        for p in range(PIECES):
            rows = pl.ds(p * step, step)
            copies.append(pltpu.make_async_copy(src.at[rows], dst.at[rows], sems.at[i, p]))
            copies[-1].start()
    return copies


def route_kernel(tok_hbm, cot_hbm, sp, send, disp, comb, tok, cot, sems):
    copies = start_pieces(((tok_hbm, tok), (cot_hbm, cot)), sems)
    for copy in copies[:PIECES]:
        copy.wait()
    logits = nt(sp[...], tok[...])
    ed = jnp.exp(logits - jnp.max(logits, axis=1, keepdims=True))
    d = ed / jnp.sum(ed, axis=1, keepdims=True)
    ec = jnp.exp(logits - jnp.max(logits, axis=0, keepdims=True))
    c = ec / jnp.sum(ec, axis=0, keepdims=True)
    disp[...] = d
    comb[...] = c
    slot_in = nn(d.astype(bf16), tok[...]).astype(bf16)
    for copy in copies[PIECES:]:
        copy.wait()
    slot_grad = nn(c.astype(bf16), cot[...]).astype(bf16)
    both = jnp.concatenate([slot_in.astype(f32), slot_grad.astype(f32)], axis=0).astype(bf16)
    rows = 2 * CHIP_COUNT
    sel = pick(rows, 16, lambda r: (r % 2) * EXPERTS + r // (2 * SPREAD))
    send[...] = nn(sel, both).astype(bf16)


def expert_kernel(place, own, other, w_in, w_out, part_own, part_other, c0, c1, c2, c3, turned):
    n = own.shape[0] // 2
    even = pick(n, 2 * n, lambda r: 2 * r)
    odd = pick(n, 2 * n, lambda r: 2 * r + 1)
    rows_in = jnp.concatenate([nn(even, own[...]), nn(even, other[...])], axis=0).astype(bf16)
    rows_grad = jnp.concatenate([nn(odd, own[...]), nn(odd, other[...])], axis=0).astype(bf16)
    preact = nn(rows_in, w_in[...])
    hidden_grad = nn(rows_grad, w_out[...])
    cumulative = 0.5 * (1.0 + lax.erf(preact * root_half))
    slope = cumulative + preact * jnp.exp(-0.5 * preact * preact) * density
    act = (preact * cumulative).astype(bf16)
    gp = (hidden_grad * slope).astype(bf16)
    out_part = nt(act, w_out[...]).astype(bf16)
    grad_part = nt(gp, w_in[...]).astype(bf16)
    part_own[...] = (tn(even, out_part[:n]) + tn(odd, grad_part[:n])).astype(bf16)
    part_other[...] = (tn(even, out_part[n:]) + tn(odd, grad_part[n:])).astype(bf16)
    both = jnp.concatenate([rows_in, rows_grad], axis=0)
    turned[...] = jnp.transpose(both.astype(f32)).astype(bf16)
    y, xl = place[0], place[1]
    depth = turned.shape[0] // 16
    for m, chunk in enumerate((c0, c1, c2, c3)):
        chunk[0 : 2 * n, :] = gp
        chunk[2 * n : 4 * n, :] = act
        there = jnp.bitwise_xor(y, 4 * (m // 2)), jnp.bitwise_xor(xl, m % 2)
        pieces = []
        for k in STEPS:
            at = (jnp.bitwise_and(there[0] + k, ROWS - 1) * 2 + there[1]) * depth
            pieces.append(turned[pl.ds(pl.multiple_of(at, 16), depth), :])
        piece = jnp.concatenate(pieces, axis=0)
        for b in range(5):
            chunk[4 * n : 6 * n, 128 * b : 128 * (b + 1)] = piece[64 * b : 64 * (b + 1)]


def term_kernel(c0, c1, c2, c3, _, keep, s1, s2, s3):
    left, right = [], []
    zero = jnp.zeros((64, 640), bf16)
    for chunk in (c0, c1, c2, c3):
        left.append(jnp.concatenate([chunk[128:192, 128 * b : 128 * (b + 1)] for b in range(5)], axis=0))
        right.append(jnp.concatenate([chunk[0:64, :], zero], axis=1))
        right.append(jnp.concatenate([zero, chunk[64:128, :]], axis=1))
    total = nn(jnp.concatenate(left, axis=1), jnp.concatenate(right, axis=0))
    depth = keep.shape[0]
    keep[...] = total[:depth]
    for k, s in enumerate((s1, s2, s3)):
        s[...] = total[(k + 1) * depth : (k + 2) * depth].astype(bf16)


def finish_kernel(tok_hbm, cot_hbm, sp, parts, disp, comb, mixed, grad_tokens, done, tok, cot, sems):
    copies = start_pieces(((tok_hbm, tok), (cot_hbm, cot)), sems)
    for copy in copies:
        copy.wait()
    done[...] = jnp.zeros_like(done)
    r = lax.broadcasted_iota(jnp.int32, (16, 2 * CHIP_COUNT), 0)
    c = lax.broadcasted_iota(jnp.int32, (16, 2 * CHIP_COUNT), 1)
    sel = jnp.where(((c % 2) * EXPERTS + c // (2 * SPREAD)) == r, 1.0, 0.0).astype(bf16)
    slots = nn(sel, parts[...])
    slot_out = slots[:8].astype(bf16)
    grad_slot_in = slots[8:].astype(bf16)
    d, cm = disp[...], comb[...]
    mixed[...] = tn(cm.astype(bf16), slot_out).astype(bf16)
    combine_grad = nt(slot_out, cot[...])
    dispatch_grad = nt(grad_slot_in, tok[...])
    lg = cm * (combine_grad - jnp.sum(cm * combine_grad, axis=0, keepdims=True))
    lg = lg + d * (dispatch_grad - jnp.sum(d * dispatch_grad, axis=1, keepdims=True))
    rows = jnp.concatenate([d.astype(bf16).astype(f32), lg.astype(bf16).astype(f32)], axis=0)
    cols = jnp.concatenate([grad_slot_in.astype(f32), sp[...].astype(f32)], axis=0)
    grad_tokens[...] = tn(rows.astype(bf16), cols.astype(bf16)).astype(bf16)


def total_kernel(keep, a, b, c, _, grad_in, grad_out):
    total = keep[...] + a[...].astype(f32) + b[...].astype(f32) + c[...].astype(f32)
    hidden = grad_in.shape[1]
    grad_in[...] = total[:, :hidden]
    grad_out[...] = total[:, hidden:]


def per_device(tokens, cotangent, slot_params, in_weight, out_weight):
    tok, cot = tokens[0], cotangent[0]
    patch, width = tok.shape
    hidden = in_weight.shape[1]
    sp = slot_params.T
    n2 = 2 * CHIP_COUNT
    send, disp, comb = call(
        route_kernel,
        [((n2, width), bf16), ((EXPERTS, patch), f32), ((EXPERTS, patch), f32)],
        10**7, 1500000, "hhv",
        [pltpu.VMEM((patch, width), bf16)] * 2 + [pltpu.SemaphoreType.DMA((2, PIECES))],
        56_000_000,
    )(tok, cot, sp)

    def exchange(rows):
        got = lax.all_to_all(rows.reshape(CHIP_COUNT, 2, width), CHIPS, 0, 0, tiled=True)
        return got.reshape(n2, width)

    swap = [(0, 1), (1, 0)]
    own = exchange(send)
    other = lax.ppermute(own, "c", swap)
    place = jnp.stack([lax.axis_index(Y), lax.axis_index("xl")]).astype(jnp.int32)
    chunk_shape = ((192, hidden), bf16)
    part_own, part_other, c0, c1, c2, c3 = call(
        expert_kernel,
        [((n2, width), bf16), ((n2, width), bf16)] + [chunk_shape] * 4,
        5 * 10**8, 4500000, "svvvv", [pltpu.VMEM((width, 128), bf16)],
    )(place, own, other, in_weight, out_weight)

    back = lax.ppermute(part_other, "c", swap)
    got = [c0]
    for m, chunk in ((3, c3), (2, c2), (1, c1)):
        got.append(lax.ppermute(chunk, QUAD, [(i, i ^ m) for i in range(QUADS)]))
    returned = (part_own.astype(f32) + back.astype(f32)).astype(bf16)
    parts = exchange(returned)

    depth = width // 16
    piece = ((depth, 2 * hidden), bf16)
    keep, s1, s2, s3 = call(
        term_kernel,
        [((depth, 2 * hidden), f32), piece, piece, piece],
        12 * 10**9, 2500000, "vvvva",
    )(*got, returned)
    shares = [
        lax.ppermute(s, Y, [(i, (i + k) % ROWS) for i in range(ROWS)]) for k, s in zip(STEPS[1:], (s1, s2, s3))
    ]

    mixed, grad_tokens, done = call(
        finish_kernel,
        [((patch, width), bf16), ((patch, width), bf16), ((8, 128), f32)],
        3 * 10**7, 3000000, "hhvvvv",
        [pltpu.VMEM((patch, width), bf16)] * 2 + [pltpu.SemaphoreType.DMA((2, PIECES))], 56_000_000,
    )(tok, cot, sp, parts, disp, comb)
    grad_in, grad_out = call(
        total_kernel, [((depth, hidden), f32)] * 2, 10**6, 1500000, "vvvva",
    )(keep, *shares, done)
    return mixed[None], grad_tokens[None], grad_in, grad_out


def solution(mesh):
    fine = Mesh(np.asarray(mesh.devices).reshape(SIZES), AXES)
    return jax.shard_map(
        per_device,
        mesh=fine,
        in_specs=(P(AXES), P(AXES), P(), P(None, PEERS), P(None, PEERS)),
        out_specs=(P(AXES), P(AXES), P(DP, PEERS), P(DP, PEERS)),
        check_vma=False,
    )
```

```python
import functools

import jax
import jax.numpy as jnp
import numpy as np
from jax import lax
from jax.experimental import pallas as pl
from jax.experimental.pallas import tpu as pltpu
from jax.sharding import Mesh
from jax.sharding import PartitionSpec as P

root_half = 0.7071067811865476
density = 0.3989422804014327
f32 = jnp.float32
bf16 = jnp.bfloat16

AXES = ("yh", "yl", "xl", "xh", "zh", "zu", "zv", "c")
SIZES = (4, 2, 2, 2, 4, 2, 2, 2)
DP = ("yh", "yl", "xl")
PEERS = ("xh", "zh", "zu", "zv", "c")
CHIPS = ("xh", "zh", "zu", "zv")
PAIRS, NEAR = ("xh", "zh", "zu"), ("zv", "c")
PAIR_COUNT = 16
QUAD = ("yl", "xl")
EXPERTS, SPREAD, CHIP_COUNT = 8, 4, 32
QUADS = 4
PIECES = 4
ROOM = 20_000_000


def nn(a, b):
    return lax.dot_general(a, b, (((1,), (0,)), ((), ())), preferred_element_type=f32)


def nt(a, b):
    return lax.dot_general(a, b, (((1,), (1,)), ((), ())), preferred_element_type=f32)


def tn(a, b):
    return lax.dot_general(a, b, (((0,), (0,)), ((), ())), preferred_element_type=f32)


def pick(rows, cols, source):
    r = lax.broadcasted_iota(jnp.int32, (rows, cols), 0)
    c = lax.broadcasted_iota(jnp.int32, (rows, cols), 1)
    return jnp.where(c == source(r), 1.0, 0.0).astype(bf16)


def call(kernel, outs, flops, nbytes, ins, scratch=(), room=ROOM):
    vm = pl.BlockSpec(memory_space=pltpu.VMEM)
    spaces = {"v": vm, "s": pl.BlockSpec(memory_space=pltpu.SMEM), "a": pl.BlockSpec(memory_space=pl.ANY)}
    spaces["h"] = pl.BlockSpec(memory_space=pltpu.HBM)
    specs = [spaces[letter] for letter in ins]
    return pl.pallas_call(
        kernel,
        out_shape=[jax.ShapeDtypeStruct(s, d) for s, d in outs],
        in_specs=specs,
        out_specs=[vm] * len(outs),
        scratch_shapes=list(scratch),
        compiler_params=pltpu.CompilerParams(vmem_limit_bytes=room),
        cost_estimate=pl.CostEstimate(flops=flops, bytes_accessed=nbytes, transcendentals=0),
    )


def start_pieces(pairs, sems):
    copies = []
    for i, (src, dst) in enumerate(pairs):
        step = dst.shape[0] // PIECES
        for p in range(PIECES):
            rows = pl.ds(p * step, step)
            copies.append(pltpu.make_async_copy(src.at[rows], dst.at[rows], sems.at[i, p]))
            copies[-1].start()
    return copies


def route_kernel(tok_hbm, cot_hbm, sp, send, disp, comb, tok, cot, sems):
    copies = start_pieces(((tok_hbm, tok), (cot_hbm, cot)), sems)
    for copy in copies[:PIECES]:
        copy.wait()
    logits = nt(sp[...], tok[...])
    ed = jnp.exp(logits - jnp.max(logits, axis=1, keepdims=True))
    d = ed / jnp.sum(ed, axis=1, keepdims=True)
    ec = jnp.exp(logits - jnp.max(logits, axis=0, keepdims=True))
    c = ec / jnp.sum(ec, axis=0, keepdims=True)
    disp[...] = d
    comb[...] = c
    slot_in = nn(d.astype(bf16), tok[...]).astype(bf16)
    for copy in copies[PIECES:]:
        copy.wait()
    slot_grad = nn(c.astype(bf16), cot[...]).astype(bf16)
    both = jnp.concatenate([slot_in.astype(f32), slot_grad.astype(f32)], axis=0).astype(bf16)
    rows = 2 * PAIR_COUNT
    sel = pick(rows, 16, lambda r: (r % 2) * EXPERTS + r // 4)
    send[...] = nn(sel, both).astype(bf16)


def expert_kernel(place, rows, w_in, w_out, part_own, part_other, c0, c1, c2, c3, turned):
    n = rows.shape[0] // 4
    even = pick(n, 2 * n, lambda r: 2 * r)
    odd = pick(n, 2 * n, lambda r: 2 * r + 1)
    take_in = pick(n, 2 * n, lambda r: (r % 2) * n + (r // 2) * 2)
    take_grad = pick(n, 2 * n, lambda r: (r % 2) * n + (r // 2) * 2 + 1)

    def of_core(core):
        at = pl.multiple_of(core * n, n)
        return jnp.concatenate([rows[pl.ds(at, n), :], rows[pl.ds(2 * n + at, n), :]], axis=0)

    own, other = of_core(place[2]), of_core(1 - place[2])
    rows_in = jnp.concatenate([nn(take_in, own), nn(take_in, other)], axis=0).astype(bf16)
    rows_grad = jnp.concatenate([nn(take_grad, own), nn(take_grad, other)], axis=0).astype(bf16)
    preact = nn(rows_in, w_in[...])
    hidden_grad = nn(rows_grad, w_out[...])
    cumulative = 0.5 * (1.0 + lax.erf(preact * root_half))
    slope = cumulative + preact * jnp.exp(-0.5 * preact * preact) * density
    act = (preact * cumulative).astype(bf16)
    gp = (hidden_grad * slope).astype(bf16)
    out_part = nt(act, w_out[...]).astype(bf16)
    grad_part = nt(gp, w_in[...]).astype(bf16)
    part_own[...] = (tn(even, out_part[:n]) + tn(odd, grad_part[:n])).astype(bf16)
    part_other[...] = (tn(even, out_part[n:]) + tn(odd, grad_part[n:])).astype(bf16)
    both = jnp.concatenate([rows_in, rows_grad], axis=0)
    turned[...] = jnp.transpose(both.astype(f32)).astype(bf16)
    yh, j0 = place[0], place[1]
    depth = turned.shape[0] // 16
    for m, chunk in enumerate((c0, c1, c2, c3)):
        chunk[0 : 2 * n, :] = gp
        chunk[2 * n : 4 * n, :] = act
        j = jnp.bitwise_xor(j0, m)
        pieces = []
        for k in range(4):
            at = (lax.rem(yh + k, 4) * QUADS + j) * depth
            pieces.append(turned[pl.ds(pl.multiple_of(at, 16), depth), :])
        piece = jnp.concatenate(pieces, axis=0)
        for b in range(5):
            chunk[4 * n : 6 * n, 128 * b : 128 * (b + 1)] = piece[64 * b : 64 * (b + 1)]


def term_kernel(c0, c1, c2, c3, _, keep, s1, s2, s3):
    left, right = [], []
    zero = jnp.zeros((64, 640), bf16)
    for chunk in (c0, c1, c2, c3):
        left.append(jnp.concatenate([chunk[128:192, 128 * b : 128 * (b + 1)] for b in range(5)], axis=0))
        right.append(jnp.concatenate([chunk[0:64, :], zero], axis=1))
        right.append(jnp.concatenate([zero, chunk[64:128, :]], axis=1))
    total = nn(jnp.concatenate(left, axis=1), jnp.concatenate(right, axis=0))
    depth = keep.shape[0]
    keep[...] = total[:depth]
    for k, s in enumerate((s1, s2, s3)):
        s[...] = total[(k + 1) * depth : (k + 2) * depth].astype(bf16)


def finish_kernel(tok_hbm, cot_hbm, sp, parts, disp, comb, mixed, grad_tokens, done, tok, cot, sems):
    copies = start_pieces(((tok_hbm, tok), (cot_hbm, cot)), sems)
    for copy in copies:
        copy.wait()
    done[...] = jnp.zeros_like(done)
    r = lax.broadcasted_iota(jnp.int32, (16, 2 * CHIP_COUNT), 0)
    c = lax.broadcasted_iota(jnp.int32, (16, 2 * CHIP_COUNT), 1)
    sel = jnp.where(((c % 2) * EXPERTS + c // (2 * SPREAD)) == r, 1.0, 0.0).astype(bf16)
    slots = nn(sel, parts[...])
    slot_out = slots[:8].astype(bf16)
    grad_slot_in = slots[8:].astype(bf16)
    d, cm = disp[...], comb[...]
    mixed[...] = tn(cm.astype(bf16), slot_out).astype(bf16)
    combine_grad = nt(slot_out, cot[...])
    dispatch_grad = nt(grad_slot_in, tok[...])
    lg = cm * (combine_grad - jnp.sum(cm * combine_grad, axis=0, keepdims=True))
    lg = lg + d * (dispatch_grad - jnp.sum(d * dispatch_grad, axis=1, keepdims=True))
    rows = jnp.concatenate([d.astype(bf16).astype(f32), lg.astype(bf16).astype(f32)], axis=0)
    cols = jnp.concatenate([grad_slot_in.astype(f32), sp[...].astype(f32)], axis=0)
    grad_tokens[...] = tn(rows.astype(bf16), cols.astype(bf16)).astype(bf16)


def total_kernel(keep, a, b, c, _, grad_in, grad_out):
    total = keep[...] + a[...].astype(f32) + b[...].astype(f32) + c[...].astype(f32)
    hidden = grad_in.shape[1]
    grad_in[...] = total[:, :hidden]
    grad_out[...] = total[:, hidden:]


def per_device(tokens, cotangent, slot_params, in_weight, out_weight):
    tok, cot = tokens[0], cotangent[0]
    patch, width = tok.shape
    hidden = in_weight.shape[1]
    sp = slot_params.T
    n2 = 2 * CHIP_COUNT
    send, disp, comb = call(
        route_kernel,
        [((2 * PAIR_COUNT, width), bf16), ((EXPERTS, patch), f32), ((EXPERTS, patch), f32)],
        10**7, 1500000, "hhv",
        [pltpu.VMEM((patch, width), bf16)] * 2 + [pltpu.SemaphoreType.DMA((2, PIECES))],
        56_000_000,
    )(tok, cot, sp)

    def exchange(rows):
        got = lax.all_to_all(rows.reshape(CHIP_COUNT, 2, width), CHIPS, 0, 0, tiled=True)
        return got.reshape(n2, width)

    swap = [(0, 1), (1, 0)]
    part = lax.all_to_all(send.reshape(PAIR_COUNT, 2, width), PAIRS, 0, 0, tiled=True)
    rows = lax.all_gather(part.reshape(2 * PAIR_COUNT, width), NEAR, tiled=True)
    place = jnp.stack([lax.axis_index("yh"), lax.axis_index(QUAD), lax.axis_index("c")]).astype(jnp.int32)
    chunk_shape = ((192, hidden), bf16)
    part_own, part_other, c0, c1, c2, c3 = call(
        expert_kernel,
        [((n2, width), bf16), ((n2, width), bf16)] + [chunk_shape] * 4,
        5 * 10**8, 4500000, "svvv", [pltpu.VMEM((width, 128), bf16)],
    )(place, rows, in_weight, out_weight)

    back = lax.ppermute(part_other, "c", swap)
    got = [c0]
    for m, chunk in ((3, c3), (1, c1), (2, c2)):
        got.append(lax.ppermute(chunk, QUAD, [(i, i ^ m) for i in range(QUADS)]))
    returned = (part_own.astype(f32) + back.astype(f32)).astype(bf16)
    parts = exchange(returned)

    depth = width // 16
    piece = ((depth, 2 * hidden), bf16)
    keep, s1, s2, s3 = call(
        term_kernel,
        [((depth, 2 * hidden), f32), piece, piece, piece],
        12 * 10**9, 2500000, "vvvva",
    )(*got, returned)
    shares = [
        lax.ppermute(s, "yh", [(i, (i + k) % 4) for i in range(4)]) for k, s in ((2, s2), (1, s1), (3, s3))
    ]

    mixed, grad_tokens, done = call(
        finish_kernel,
        [((patch, width), bf16), ((patch, width), bf16), ((8, 128), f32)],
        3 * 10**7, 3000000, "hhvvvv",
        [pltpu.VMEM((patch, width), bf16)] * 2 + [pltpu.SemaphoreType.DMA((2, PIECES))], 56_000_000,
    )(tok, cot, sp, parts, disp, comb)
    grad_in, grad_out = call(
        total_kernel, [((depth, hidden), f32)] * 2, 10**6, 1500000, "vvvva",
    )(keep, *shares, done)
    return mixed[None], grad_tokens[None], grad_in, grad_out


def solution(mesh):
    fine = Mesh(np.asarray(mesh.devices).reshape(SIZES), AXES)
    return jax.shard_map(
        per_device,
        mesh=fine,
        in_specs=(P(AXES), P(AXES), P(), P(None, PEERS), P(None, PEERS)),
        out_specs=(P(AXES), P(AXES), P(DP, PEERS), P(DP, PEERS)),
        check_vma=False,
    )
```
